256 devices in a mesh: pair: 2 (over y_hi), tm: 8 (over z), fsdp: 16 (over y_lo, x, core).
Axes of the slice: x: 4, y: 4 (y_hi: 2, y_lo: 2; y = y_hi * 2 + y_lo), z: 8, core: 2. Of those that a mesh axis runs over, the one named last changes fastest.
Arguments:
- frames: bfloat16 [2, 64, 1024, 1536], P('pair', 'tm', 'fsdp'), may hold values from -8 to 8
- frame_time: int32 [2, 64], P('pair'), may hold values from 0 to 63, as said below
- w_qkv: bfloat16 [1536, 2304], P('fsdp'), may hold values from -1 to 1
- w_out: bfloat16 [768, 1536], P(None, 'fsdp'), may hold values from -0.21875 to 0.21875
- grad_out: bfloat16 [2, 64, 1024, 1536], P('pair', 'tm', 'fsdp'), may hold values from -6 to 6
Outputs:
- grad_frames: bfloat16 [2, 64, 1024, 1536], P('pair', 'tm', 'fsdp')
- grad_qkv: float32 [1536, 2304], P('fsdp')
- grad_out_weight: float32 [768, 1536], P(None, 'fsdp')
The draws below stay inside these ranges and needn't reach their ends.
Inputs may be any that keep to these rules, and one draw needn't show every extreme that they name: `frame_time`: Non-decreasing along the frames of a clip, 0 at its first frame and 63 at its last; equal values mark frames of one time step.
All inputs are finite; a program needn't handle non-finite values.
Results may differ from the reference program's by a relative error of at most 0.04.
The reference program's roundings to bfloat16 on the way count: a program that leaves them out, or rounds other values in their place, can miss the bound.
Values may be sent and summed in bfloat16 or wider, within the bound.
No kernel may reach another device: no remote copies, remote signals or barrier semaphores. Data moves between devices by JAX's collectives and lax.ppermute only.
A program may use at most 128 MiB of HBM per device.

```python
import math
import jax
import jax.numpy as jnp
from jax import lax

D = 1536
HEADS = 12
HEAD_DIM = 64
F_DEV = 8
P_DEV = 64
FRAMES = 64
PATCHES = 1024
CLIPS = 2
TOKENS = 131072
N_TM = 8
N_FSDP = 16


def draw_frames(key, part):
    key = jax.random.fold_in(key, 11)
    first_key = jax.random.fold_in(key, 0)
    full_shape = (CLIPS, FRAMES, PATCHES, D)
    sample = jax.random.normal(first_key, full_shape, jnp.float32)
    return jnp.clip(sample, -8.0, 8.0).astype(jnp.bfloat16)


def draw_frame_time(key, part):
    key = jax.random.fold_in(key, 23)
    drawn = jax.random.randint(key, (CLIPS, FRAMES), 0, FRAMES, jnp.int32)
    position = jnp.arange(FRAMES, dtype=jnp.int32)[None, :]
    drawn = jnp.where(position == 0, 0, drawn)
    drawn = jnp.where(position == FRAMES - 1, FRAMES - 1, drawn)
    return jnp.sort(drawn, axis=1).astype(jnp.int32)


def draw_w_qkv(key, part):
    key = jax.random.fold_in(key, 37)
    first_key = jax.random.fold_in(key, 0)
    base_draw = jax.random.normal(first_key, (D, 3, HEADS, HEAD_DIM), jnp.float32) * D ** (-0.5)
    stacked = base_draw
    return jnp.clip(stacked.reshape(D, 3 * HEADS * HEAD_DIM), -1.0, 1.0).astype(jnp.bfloat16)


def with_spikes(values, rng, source, target, shards_of, factor):
    def block_of(dim):
        return (jnp.arange(values.shape[dim]) // (values.shape[dim] // shards_of)).reshape((-1,) + (1,) * (values.ndim - 1 - dim))

    first = jax.random.permutation(rng, shards_of)[block_of(target)]
    second = (block_of(target) + shards_of // 2) % shards_of
    return jnp.where((block_of(source) == first) | (block_of(source) == second), factor * values, values)


def levels(rng, shape, shards, low, high):
    loudness = 1.0
    for dim, parts in shards:
        heights = jax.random.uniform(jax.random.fold_in(jax.random.fold_in(rng, 6), dim), (parts,), jnp.float32, low / len(shards), high / len(shards))
        loudness = loudness * jnp.repeat(jnp.exp(heights), shape[dim] // parts).reshape((-1,) + (1,) * (len(shape) - 1 - dim))
    return loudness


def scatter_about(stream_key, dims, spread, limit, cuts=(), kind=jnp.bfloat16):
    entries = spread * jax.random.normal(stream_key, dims, jnp.float32)
    if cuts:
        entries = entries * levels(stream_key, dims, cuts, -0.22, 0.18)
    return jnp.clip(entries, -limit, limit).astype(kind)


def gaussian_with(rng, shape, spread, reach, pieces, heavy, kind=jnp.bfloat16):
    result = spread * jax.random.normal(rng, shape, jnp.float32)
    if pieces:
        result = result * levels(rng, shape, pieces, -0.22, 0.18)
    return jnp.clip(with_spikes(result, jax.random.fold_in(rng, 3), *heavy), -reach, reach).astype(kind)


def setup_inputs(seed: int = 0) -> dict:
    splits = jax.random.split(jax.random.key(seed), 6)
    return {
        "frames": draw_frames(jax.random.fold_in(splits[5], 71), 0),
        "frame_time": draw_frame_time(jax.random.fold_in(splits[5], 71), 0),
        "w_qkv": draw_w_qkv(jax.random.fold_in(splits[5], 71), 0),
        "w_out": scatter_about(splits[3], (HEADS * HEAD_DIM, D), (HEADS * HEAD_DIM) ** -0.5, 0.21875, ((1, 16),)),
        "grad_out": gaussian_with(splits[4], (CLIPS, FRAMES, PATCHES, D), 1.0, 6.0, ((0, 2), (1, 8), (2, 16)), (2, 3, 16, 2.0)),
    }


def norm_parts(frames_in):
    float_rows = frames_in.astype(jnp.float32)
    inv_rms = lax.rsqrt(lax.optimization_barrier(jnp.mean(float_rows * float_rows, axis=-1, keepdims=True)) + 1e-06)
    normed = (float_rows * inv_rms).astype(jnp.bfloat16)
    return (float_rows, inv_rms, normed)

def attention_forward(qkv, frame_times):
    clips_here, frames_here, patches_here, triple = qkv.shape
    head_count = triple // (3 * HEAD_DIM)
    split_qkv = qkv.reshape(clips_here, frames_here, patches_here, 3, head_count, HEAD_DIM).astype(jnp.float32)
    queries = split_qkv[:, :, :, 0]
    key_rows = split_qkv[:, :, :, 1]
    values = split_qkv[:, :, :, 2]
    scores = jnp.einsum('ciphd,cjphd->cphij', queries, key_rows) * HEAD_DIM ** (-0.5)
    allowed = frame_times[:, None, :] <= frame_times[:, :, None]
    scores = jnp.where(allowed[:, None, None, :, :], scores, -1e+30)
    row_max = lax.optimization_barrier(jnp.max(scores, axis=-1, keepdims=True))
    exponent = jnp.exp(scores - row_max)
    weights = exponent / lax.optimization_barrier(jnp.sum(exponent, axis=-1, keepdims=True))
    rounded_weights = weights.astype(jnp.bfloat16)
    mixed_rows = jnp.einsum('cphij,cjphd->ciphd', rounded_weights.astype(jnp.float32), values).astype(jnp.bfloat16)
    mixed_rows = mixed_rows.reshape(clips_here, frames_here, patches_here, head_count * HEAD_DIM)
    return (mixed_rows, weights, rounded_weights, split_qkv)

def attention_backward(d_mixed, weights, rounded_weights, split_qkv):
    clips_here, frames_here, patches_here, inner_width = d_mixed.shape
    head_count = inner_width // HEAD_DIM
    d_heads = d_mixed.reshape(clips_here, frames_here, patches_here, head_count, HEAD_DIM).astype(jnp.float32)
    queries = split_qkv[:, :, :, 0]
    key_rows = split_qkv[:, :, :, 1]
    values = split_qkv[:, :, :, 2]
    d_weights = jnp.einsum('ciphd,cjphd->cphij', d_heads, values)
    centered = d_weights - lax.optimization_barrier(jnp.sum(weights * d_weights, axis=-1, keepdims=True))
    d_scores = (weights * centered * HEAD_DIM ** (-0.5)).astype(jnp.bfloat16).astype(jnp.float32)
    d_query = jnp.einsum('cphij,cjphd->ciphd', d_scores, key_rows).astype(jnp.bfloat16)
    d_key = jnp.einsum('cphij,ciphd->cjphd', d_scores, queries).astype(jnp.bfloat16)
    d_value = jnp.einsum('cphij,ciphd->cjphd', rounded_weights.astype(jnp.float32), d_heads).astype(jnp.bfloat16)
    stacked = jnp.stack([d_query, d_key, d_value], axis=3)
    return stacked.reshape(clips_here, frames_here, patches_here, 3 * inner_width)

def norm_backward(d_normed, float_rows, inv_rms, grad_rows):
    scaled = float_rows * inv_rms
    inner_term = lax.optimization_barrier(jnp.mean(d_normed * scaled, axis=-1, keepdims=True))
    return (grad_rows.astype(jnp.float32) + inv_rms * (d_normed - scaled * inner_term)).astype(jnp.bfloat16)

def reference(frames, frame_time, w_qkv, w_out, grad_out):
    inner_width = w_out.shape[0]
    block_rows = F_DEV * P_DEV
    grad_scale = 1.0 / math.sqrt(TOKENS)

    def per_clip(totals, clip_item):
        clip_frames, clip_times, clip_grad = clip_item
        frame_blocks = clip_frames.reshape(FRAMES, N_FSDP, P_DEV, D).transpose(1, 0, 2, 3)
        grad_blocks = clip_grad.reshape(FRAMES, N_FSDP, P_DEV, D).transpose(1, 0, 2, 3)

        def per_patches(sums, patch_item):
            block_frames, block_grad = patch_item
            float_rows, inv_rms, normed = norm_parts(block_frames)
            flat_normed = normed.reshape(-1, D)
            qkv = jnp.dot(flat_normed, w_qkv, preferred_element_type=jnp.float32).astype(jnp.bfloat16)
            qkv = qkv.reshape(1, FRAMES, P_DEV, 3 * inner_width)
            mixed_rows, weights, rounded_weights, split_qkv = attention_forward(qkv, clip_times[None])
            grad_rows = block_grad.reshape(-1, D)
            d_mixed = jnp.dot(grad_rows, w_out.T, preferred_element_type=jnp.float32).astype(jnp.bfloat16)
            d_mixed = d_mixed.reshape(1, FRAMES, P_DEV, inner_width)
            d_qkv = attention_backward(d_mixed, weights, rounded_weights, split_qkv).reshape(-1, 3 * inner_width)
            d_normed = jnp.dot(d_qkv, w_qkv.T, preferred_element_type=jnp.float32)
            grad_piece = norm_backward(d_normed.reshape(FRAMES, P_DEV, D), float_rows, inv_rms, block_grad)
            mixed_flat = mixed_rows.reshape(-1, inner_width)

            def per_block(inner_sums, block_index):
                first_row = block_index * block_rows
                normed_block = lax.dynamic_slice_in_dim(flat_normed, first_row, block_rows, 0)
                dqkv_block = lax.dynamic_slice_in_dim(d_qkv, first_row, block_rows, 0)
                mixed_block = lax.dynamic_slice_in_dim(mixed_flat, first_row, block_rows, 0)
                grad_block = lax.dynamic_slice_in_dim(grad_rows, first_row, block_rows, 0)
                term_qkv = jnp.dot(normed_block.T, dqkv_block, preferred_element_type=jnp.float32)
                term_out = jnp.dot(mixed_block.T, grad_block, preferred_element_type=jnp.float32)
                term_qkv = lax.optimization_barrier(term_qkv.astype(jnp.bfloat16)).astype(jnp.float32)
                term_out = lax.optimization_barrier(term_out.astype(jnp.bfloat16)).astype(jnp.float32)
                return ((inner_sums[0] + term_qkv, inner_sums[1] + term_out), None)
            sums, unused = lax.scan(per_block, sums, jnp.arange(N_TM, dtype=jnp.int32))
            return (sums, grad_piece)
        totals, grad_pieces = lax.scan(per_patches, totals, (frame_blocks, grad_blocks))
        grad_clip = grad_pieces.transpose(1, 0, 2, 3).reshape(FRAMES, PATCHES, D)
        return (totals, grad_clip)
    start_sums = (jnp.zeros((D, 3 * inner_width), jnp.float32), jnp.zeros((inner_width, D), jnp.float32))
    totals, grad_frames = lax.scan(per_clip, start_sums, (frames, frame_time, grad_out))
    return (grad_frames, totals[0] * grad_scale, totals[1] * grad_scale)
```

```python
import math

import jax
import jax.numpy as jnp
import numpy as np
from jax import lax
from jax.experimental import pallas as pl
from jax.experimental.pallas import tpu as pltpu
from jax.sharding import Mesh
from jax.sharding import PartitionSpec as P

HEAD_DIM = 64
FSDP = ("yl", "x", "core")
GROUP = ("pair", "tm")
MASKED = -1e30
VMEM_BYTES = 48 * 1024 * 1024


def low_half(rows):
    return lax.broadcasted_iota(jnp.int32, (rows, 2 * HEAD_DIM), 1) < HEAD_DIM


def stack_heads(pair_rows):
    first = low_half(pair_rows.shape[0])
    zero = jnp.zeros_like(pair_rows)
    return jnp.concatenate([jnp.where(first, pair_rows, zero), jnp.where(first, zero, pair_rows)], axis=0)


def merge_heads(stacked):
    rows = stacked.shape[0] // 2
    return jnp.where(low_half(rows), stacked[:rows], stacked[rows:])


def contract(left, right, left_dim, right_dim):
    return lax.dot_general(
        left, right, (((left_dim,), (right_dim,)), ((), ())), preferred_element_type=jnp.float32
    )


def forward_kernel(mask_ref, qkv_ref, mixed_ref, weights_ref):
    wide = 2 * HEAD_DIM
    inner = mixed_ref.shape[-1]
    rows = mask_ref.shape[1]
    allowed = mask_ref[...] > 0.5
    for pair in range(inner // wide):
        first = pair * wide
        queries = stack_heads(qkv_ref[..., first : first + wide].reshape(rows, wide))
        keys = qkv_ref[..., inner + first : inner + first + wide].reshape(rows, wide)
        values = qkv_ref[..., 2 * inner + first : 2 * inner + first + wide].reshape(rows, wide)
        scores = contract(queries, keys, 1, 1) * HEAD_DIM ** (-0.5)
        scores = jnp.where(allowed, scores, MASKED)
        exponent = jnp.exp(scores - jnp.max(scores, axis=-1, keepdims=True))
        weights = exponent / jnp.sum(exponent, axis=-1, keepdims=True)
        weights_ref[0, pair] = weights
        mixed = merge_heads(contract(weights.astype(jnp.bfloat16), values, 1, 0))
        mixed_ref[..., first : first + wide] = mixed.astype(jnp.bfloat16).reshape(
            mixed_ref.shape[:-1] + (wide,)
        )


def backward_kernel(qkv_ref, d_mixed_ref, weights_ref, d_qkv_ref):
    wide = 2 * HEAD_DIM
    inner = d_mixed_ref.shape[-1]
    rows = weights_ref.shape[-1]
    block = d_mixed_ref.shape[:-1] + (wide,)
    for pair in range(inner // wide):
        first = pair * wide
        queries = stack_heads(qkv_ref[..., first : first + wide].reshape(rows, wide))
        keys = qkv_ref[..., inner + first : inner + first + wide].reshape(rows, wide)
        values = qkv_ref[..., 2 * inner + first : 2 * inner + first + wide].reshape(rows, wide)
        d_heads = stack_heads(d_mixed_ref[..., first : first + wide].reshape(rows, wide))
        weights = weights_ref[0, pair]
        d_weights = contract(d_heads, values, 1, 1)
        centered = d_weights - jnp.sum(weights * d_weights, axis=-1, keepdims=True)
        d_scores = (weights * centered * HEAD_DIM ** (-0.5)).astype(jnp.bfloat16)
        d_query = merge_heads(contract(d_scores, keys, 1, 0))
        d_key = contract(d_scores, queries, 0, 0)
        d_value = contract(weights.astype(jnp.bfloat16), d_heads, 0, 0)
        for place, value in enumerate((d_query, d_key, d_value)):
            start = place * inner + first
            d_qkv_ref[..., start : start + wide] = value.astype(jnp.bfloat16).reshape(block)


def attention_forward(qkv, mask, inner):
    senders, patches, frames_each, triple = qkv.shape
    groups = patches // 2
    rows = senders * 2 * frames_each
    pairs = inner // (2 * HEAD_DIM)
    return pl.pallas_call(
        forward_kernel,
        grid=(groups,),
        in_specs=[
            pl.BlockSpec((2 * rows, rows), lambda g: (0, 0)),
            pl.BlockSpec((senders, 2, frames_each, triple), lambda g: (0, g, 0, 0)),
        ],
        out_specs=[
            pl.BlockSpec((senders, 2, frames_each, inner), lambda g: (0, g, 0, 0)),
            pl.BlockSpec((1, pairs, 2 * rows, rows), lambda g: (g, 0, 0, 0)),
        ],
        out_shape=[
            jax.ShapeDtypeStruct((senders, patches, frames_each, inner), jnp.bfloat16),
            jax.ShapeDtypeStruct((groups, pairs, 2 * rows, rows), jnp.float32),
        ],
        compiler_params=pltpu.CompilerParams(vmem_limit_bytes=VMEM_BYTES),
        cost_estimate=pl.CostEstimate(
            flops=groups * pairs * 2 * 2 * rows * rows * 256,
            bytes_accessed=8 * 1024 * 1024,
            transcendentals=groups * pairs * 2 * rows * rows,
        ),
    )(mask, qkv)


def attention_backward(qkv, d_mixed, weights):
    senders, patches, frames_each, inner = d_mixed.shape
    groups, pairs, double_rows, rows = weights.shape
    return pl.pallas_call(
        backward_kernel,
        grid=(groups,),
        in_specs=[
            pl.BlockSpec((senders, 2, frames_each, 3 * inner), lambda g: (0, g, 0, 0)),
            pl.BlockSpec((senders, 2, frames_each, inner), lambda g: (0, g, 0, 0)),
            pl.BlockSpec((1, pairs, double_rows, rows), lambda g: (g, 0, 0, 0)),
        ],
        out_specs=pl.BlockSpec((senders, 2, frames_each, 3 * inner), lambda g: (0, g, 0, 0)),
        out_shape=jax.ShapeDtypeStruct((senders, patches, frames_each, 3 * inner), jnp.bfloat16),
        compiler_params=pltpu.CompilerParams(vmem_limit_bytes=VMEM_BYTES),
        cost_estimate=pl.CostEstimate(
            flops=groups * pairs * 4 * 2 * rows * rows * 256,
            bytes_accessed=10 * 1024 * 1024,
            transcendentals=0,
        ),
    )(qkv, d_mixed, weights)


def to_patch_owner(block):
    frames_each, patches_here, width = block.shape[1:]
    owners = lax.axis_size("tm")
    split = block.reshape(frames_each, owners, patches_here // owners, width)
    return lax.all_to_all(
        split.transpose(1, 2, 0, 3), "tm", split_axis=0, concat_axis=0, tiled=True
    )


def to_frame_owner(block):
    owners, patches_each, frames_each, width = block.shape
    back = lax.all_to_all(block, "tm", split_axis=0, concat_axis=0, tiled=True)
    return back.transpose(2, 0, 1, 3).reshape(1, frames_each, owners * patches_each, width)


def attention_mask(frame_time, senders, frames_each):
    rows = np.arange(senders * 2 * frames_each)
    patch = (rows // frames_each) % 2
    frame = (rows // (2 * frames_each)) * frames_each + rows % frames_each
    times = frame_time[0][frame]
    allowed = (times[None, :] <= times[:, None]) & (patch[None, :] == patch[:, None])
    allowed = allowed.astype(jnp.float32)
    return jnp.concatenate([allowed, allowed], axis=0)


def sum_over_group(shard):
    rows, width = shard.shape
    pairs, times = lax.axis_size("pair"), lax.axis_size("tm")
    parts = shard.reshape(pairs, rows // pairs, times, width // times).transpose(0, 2, 1, 3)
    parts = parts.reshape(pairs * times, rows // pairs, width // times)
    received = lax.all_to_all(parts, GROUP, split_axis=0, concat_axis=0, tiled=True)
    mine = jnp.sum(received.astype(jnp.float32), axis=0).astype(jnp.bfloat16)
    spread = jnp.broadcast_to(mine[None], parts.shape)
    whole = lax.all_to_all(spread, GROUP, split_axis=0, concat_axis=0, tiled=True)
    whole = whole.reshape(pairs, times, rows // pairs, width // times).transpose(0, 2, 1, 3)
    return whole.reshape(rows, width)


def on_device(frames, frame_time, w_qkv, w_out, grad_out):
    inner = w_out.shape[0]
    width = frames.shape[-1]
    gathered = lax.all_gather(
        jnp.concatenate([w_qkv, w_out.T], axis=1), FSDP, axis=0, tiled=True
    )
    full_qkv = gathered[:, : 3 * inner]
    full_out_t = gathered[:, 3 * inner :]
    tokens = to_patch_owner(frames)
    grad_tokens = to_patch_owner(grad_out)
    token_shape = tokens.shape
    senders, patches_each, frames_each = token_shape[:3]
    mask = attention_mask(frame_time, senders, frames_each)

    float_rows = tokens.reshape(-1, width).astype(jnp.float32)
    inv_rms = lax.rsqrt(jnp.mean(float_rows * float_rows, axis=-1, keepdims=True) + 1e-06)
    normed = (float_rows * inv_rms).astype(jnp.bfloat16)
    qkv = jnp.dot(normed, full_qkv, preferred_element_type=jnp.float32).astype(jnp.bfloat16)
    qkv = qkv.reshape(token_shape[:3] + (3 * inner,))
    mixed, weights = attention_forward(qkv, mask, inner)

    grad_rows = grad_tokens.reshape(-1, width)
    d_mixed = jnp.dot(grad_rows, full_out_t, preferred_element_type=jnp.float32).astype(jnp.bfloat16)
    d_qkv = attention_backward(qkv, d_mixed.reshape(token_shape[:3] + (inner,)), weights)
    d_rows = d_qkv.reshape(-1, 3 * inner)

    term = jnp.concatenate(
        [
            contract(normed, d_rows, 0, 0).astype(jnp.bfloat16),
            contract(grad_rows, mixed.reshape(-1, inner), 0, 0).astype(jnp.bfloat16),
        ],
        axis=1,
    )
    shard = lax.psum_scatter(term, FSDP, scatter_dimension=0, tiled=True)

    d_normed = contract(d_rows, full_qkv, 1, 1)
    scaled = float_rows * inv_rms
    inner_term = jnp.mean(d_normed * scaled, axis=-1, keepdims=True)
    grad_local = grad_rows.astype(jnp.float32) + inv_rms * (d_normed - scaled * inner_term)
    grad_frames = to_frame_owner(grad_local.astype(jnp.bfloat16).reshape(token_shape))

    summed = sum_over_group(shard).astype(jnp.float32)
    tokens_all = frames.shape[0] * frames.shape[1] * frames.shape[2]
    for axis in GROUP + FSDP:
        tokens_all *= lax.axis_size(axis)
    scaled_sum = summed * (1.0 / math.sqrt(tokens_all))
    return (grad_frames, scaled_sum[:, : 3 * inner], scaled_sum[:, 3 * inner :].T)


def solution(mesh):
    pairs, times, shards = (mesh.shape[name] for name in ("pair", "tm", "fsdp"))
    cut = Mesh(
        mesh.devices.reshape(pairs, times, 2, shards // 4, 2), ("pair", "tm") + FSDP
    )
    tokens_spec = P("pair", "tm", FSDP, None)
    return jax.shard_map(
        on_device,
        mesh=cut,
        in_specs=(tokens_spec, P("pair", None), P(FSDP, None), P(None, FSDP), tokens_spec),
        out_specs=(tokens_spec, P(FSDP, None), P(None, FSDP)),
        check_vma=False,
    )
```

```python
import functools
import math

import jax
import jax.numpy as jnp
import numpy as np
from jax import lax
from jax.experimental import pallas as pl
from jax.experimental.pallas import tpu as pltpu
from jax.sharding import Mesh
from jax.sharding import PartitionSpec as P

HEAD_DIM = 64
FSDP = ("yl", "x", "core")
GROUP = ("pair", "tm")
MASKED = -1e30
VMEM_BYTES = 48 * 1024 * 1024


def low_half(rows):
    return lax.broadcasted_iota(jnp.int32, (rows, 2 * HEAD_DIM), 1) < HEAD_DIM


def stack_heads(pair_rows):
    first = low_half(pair_rows.shape[0])
    zero = jnp.zeros_like(pair_rows)
    return jnp.concatenate([jnp.where(first, pair_rows, zero), jnp.where(first, zero, pair_rows)], axis=0)


def merge_heads(stacked):
    rows = stacked.shape[0] // 2
    return jnp.where(low_half(rows), stacked[:rows], stacked[rows:])


def contract(left, right, left_dim, right_dim):
    return lax.dot_general(
        left, right, (((left_dim,), (right_dim,)), ((), ())), preferred_element_type=jnp.float32
    )


def forward_kernel(mask_ref, qkv_ref, mixed_ref, weights_ref):
    wide = 2 * HEAD_DIM
    inner = mixed_ref.shape[-1]
    rows = mask_ref.shape[1]
    allowed = mask_ref[...] > 0.5
    for pair in range(inner // wide):
        first = pair * wide
        queries = stack_heads(qkv_ref[..., first : first + wide].reshape(rows, wide))
        keys = qkv_ref[..., inner + first : inner + first + wide].reshape(rows, wide)
        values = qkv_ref[..., 2 * inner + first : 2 * inner + first + wide].reshape(rows, wide)
        scores = contract(queries, keys, 1, 1) * HEAD_DIM ** (-0.5)
        scores = jnp.where(allowed, scores, MASKED)
        exponent = jnp.exp(scores - jnp.max(scores, axis=-1, keepdims=True))
        weights = exponent / jnp.sum(exponent, axis=-1, keepdims=True)
        weights_ref[0, pair] = weights
        mixed = merge_heads(contract(weights.astype(jnp.bfloat16), values, 1, 0))
        mixed_ref[..., first : first + wide] = mixed.astype(jnp.bfloat16).reshape(
            mixed_ref.shape[:-1] + (wide,)
        )


def backward_kernel(qkv_ref, d_mixed_ref, weights_ref, *d_qkv_refs):
    d_qkv_ref = d_qkv_refs[-1]
    wide = 2 * HEAD_DIM
    inner = d_mixed_ref.shape[-1]
    rows = weights_ref.shape[-1]
    block = d_mixed_ref.shape[:-1] + (wide,)
    for pair in range(inner // wide):
        first = pair * wide
        queries = stack_heads(qkv_ref[..., first : first + wide].reshape(rows, wide))
        keys = qkv_ref[..., inner + first : inner + first + wide].reshape(rows, wide)
        values = qkv_ref[..., 2 * inner + first : 2 * inner + first + wide].reshape(rows, wide)
        d_heads = stack_heads(d_mixed_ref[..., first : first + wide].reshape(rows, wide))
        weights = weights_ref[0, pair]
        d_weights = contract(d_heads, values, 1, 1)
        centered = d_weights - jnp.sum(weights * d_weights, axis=-1, keepdims=True)
        d_scores = (weights * centered * HEAD_DIM ** (-0.5)).astype(jnp.bfloat16)
        d_query = merge_heads(contract(d_scores, keys, 1, 0))
        d_key = contract(d_scores, queries, 0, 0)
        d_value = contract(weights.astype(jnp.bfloat16), d_heads, 0, 0)
        for place, value in enumerate((d_query, d_key, d_value)):
            start = place * inner + first
            d_qkv_ref[..., start : start + wide] = value.astype(jnp.bfloat16).reshape(block)


def attention_forward(qkv, mask, inner):
    senders, patches, frames_each, triple = qkv.shape
    groups = patches // 2
    rows = senders * 2 * frames_each
    pairs = inner // (2 * HEAD_DIM)
    return pl.pallas_call(
        forward_kernel,
        grid=(groups,),
        in_specs=[
            pl.BlockSpec((2 * rows, rows), lambda g: (0, 0)),
            pl.BlockSpec((senders, 2, frames_each, triple), lambda g: (0, g, 0, 0)),
        ],
        out_specs=[
            pl.BlockSpec((senders, 2, frames_each, inner), lambda g: (0, g, 0, 0)),
            pl.BlockSpec((1, pairs, 2 * rows, rows), lambda g: (g, 0, 0, 0)),
        ],
        out_shape=[
            jax.ShapeDtypeStruct((senders, patches, frames_each, inner), jnp.bfloat16),
            jax.ShapeDtypeStruct((groups, pairs, 2 * rows, rows), jnp.float32),
        ],
        compiler_params=pltpu.CompilerParams(vmem_limit_bytes=VMEM_BYTES),
        cost_estimate=pl.CostEstimate(
            flops=groups * pairs * 2 * 2 * rows * rows * 256,
            bytes_accessed=8 * 1024 * 1024,
            transcendentals=groups * pairs * 2 * rows * rows,
        ),
    )(mask, qkv)


def attention_backward(qkv, d_mixed, weights, d_qkv, first, groups):
    senders, patches, frames_each, inner = d_mixed.shape
    unused, pairs, double_rows, rows = weights.shape
    given = () if d_qkv is None else (d_qkv,)
    rows_spec = lambda width: pl.BlockSpec((senders, 2, frames_each, width), lambda g: (0, g + first, 0, 0))
    return pl.pallas_call(
        backward_kernel,
        grid=(groups,),
        in_specs=[
            rows_spec(3 * inner),
            rows_spec(inner),
            pl.BlockSpec((1, pairs, double_rows, rows), lambda g: (g + first, 0, 0, 0)),
        ]
        + [ANYWHERE] * len(given),
        out_specs=rows_spec(3 * inner),
        out_shape=jax.ShapeDtypeStruct(qkv.shape, jnp.bfloat16),
        input_output_aliases={3: 0} if given else {},
        compiler_params=pltpu.CompilerParams(vmem_limit_bytes=VMEM_BYTES),
        cost_estimate=pl.CostEstimate(
            flops=groups * pairs * 4 * 2 * rows * rows * 256,
            bytes_accessed=groups * 2 * 1024 * 1024,
            transcendentals=0,
        ),
    )(qkv, d_mixed, weights, *given)


def shift_over(value, axis, step):
    count = lax.axis_size(axis)
    return lax.ppermute(value, axis, [(i, (i + step) % count) for i in range(count)])


def far_first(count):
    return sorted(range(1, count), key=lambda step: -min(step, count - step))


def split_kernel(me_ref, rows_ref, *part_refs):
    frames_each, owners, patches_each, width = rows_ref.shape
    count = frames_each * patches_each
    out_row = lax.broadcasted_iota(jnp.int32, (count, count), 0)
    in_row = lax.broadcasted_iota(jnp.int32, (count, count), 1)
    source = (out_row % frames_each) * patches_each + out_row // frames_each
    turn = (in_row == source).astype(jnp.bfloat16)
    for step, part_ref in enumerate(part_refs):
        part = rows_ref[:, lax.rem(me_ref[0] + step, owners)].reshape(count, width)
        turned = jnp.dot(turn, part, preferred_element_type=jnp.float32).astype(jnp.bfloat16)
        part_ref[...] = turned.reshape(part_ref.shape)


def project_kernel(steps, me_ref, *refs):
    owners = len(steps)
    part_refs = refs[:owners]
    weight_ref, rows_ref, product_ref, sems = refs[owners:]
    width = rows_ref.shape[-1]

    @pl.when(pl.program_id(0) == 0)
    def _():
        copies = []
        for step, part_ref in zip(steps, part_refs):
            place = lax.rem(me_ref[0] + owners - step, owners)
            copies.append(pltpu.make_async_copy(part_ref, rows_ref.at[place], sems.at[step]))
        for copy in copies:
            copy.start()
        for copy in copies:
            copy.wait()

    product = jnp.dot(
        rows_ref[...].reshape(-1, width), weight_ref[...], preferred_element_type=jnp.float32
    )
    product_ref[...] = product.astype(jnp.bfloat16).reshape(product_ref.shape)


IN_SMEM = pl.BlockSpec(memory_space=pltpu.SMEM)
IN_VMEM = pl.BlockSpec(memory_space=pltpu.VMEM)
ANYWHERE = pl.BlockSpec(memory_space=pl.ANY)


def after(value, *others):
    return lax.optimization_barrier((value,) + others)[0]


def parts_to_patch_owners(block):
    frames_each, patches_here, width = block.shape[1:]
    owners = lax.axis_size("tm")
    part = jax.ShapeDtypeStruct((patches_here // owners, frames_each, width), block.dtype)
    parts = pl.pallas_call(
        split_kernel,
        in_specs=[IN_SMEM, IN_VMEM],
        out_specs=[IN_VMEM] * owners,
        out_shape=[part] * owners,
        compiler_params=pltpu.CompilerParams(vmem_limit_bytes=VMEM_BYTES),
        cost_estimate=pl.CostEstimate(flops=2 * 64 * block.size, bytes_accessed=4 * block.size, transcendentals=0),
    )(lax.axis_index("tm").reshape(1), block.reshape(frames_each, owners, patches_here // owners, width))
    steps = far_first(owners)
    return [parts[0]] + [shift_over(parts[step], "tm", step) for step in steps], (0, *steps)


def to_patch_owner(block):
    frames_each, patches_here, width = block.shape[1:]
    owners = lax.axis_size("tm")
    split = block.reshape(frames_each, owners, patches_here // owners, width)
    return lax.all_to_all(split.transpose(1, 2, 0, 3), "tm", split_axis=0, concat_axis=0, tiled=True)


def project(parts, steps, gathered, first, columns):
    owners = len(parts)
    patches_each, frames_each, width = parts[0].shape
    token_shape = (owners, patches_each, frames_each)
    block = 256
    return pl.pallas_call(
        functools.partial(project_kernel, steps),
        grid=(columns // block,),
        in_specs=[IN_SMEM]
        + [ANYWHERE] * owners
        + [pl.BlockSpec((width, block), lambda j: (0, j + first // block))],
        out_specs=[
            pl.BlockSpec(token_shape + (width,), lambda j: (0, 0, 0, 0)),
            pl.BlockSpec(token_shape + (block,), lambda j: (0, 0, 0, j)),
        ],
        out_shape=[
            jax.ShapeDtypeStruct(token_shape + (width,), jnp.bfloat16),
            jax.ShapeDtypeStruct(token_shape + (columns,), jnp.bfloat16),
        ],
        scratch_shapes=[pltpu.SemaphoreType.DMA((owners,))],
        compiler_params=pltpu.CompilerParams(vmem_limit_bytes=VMEM_BYTES),
        cost_estimate=pl.CostEstimate(
            flops=2 * 512 * width * columns, bytes_accessed=2 * width * columns, transcendentals=0
        ),
    )(lax.axis_index("tm").reshape(1), *parts, gathered)


def to_frame_owner(block):
    owners, patches_each, frames_each, width = block.shape
    back = lax.all_to_all(block, "tm", split_axis=0, concat_axis=0, tiled=True)
    return back.transpose(2, 0, 1, 3).reshape(1, frames_each, owners * patches_each, width)


def attention_mask(frame_time, senders, frames_each):
    rows = np.arange(senders * 2 * frames_each)
    patch = (rows // frames_each) % 2
    frame = (rows // (2 * frames_each)) * frames_each + rows % frames_each
    times = frame_time[0][frame]
    allowed = (times[None, :] <= times[:, None]) & (patch[None, :] == patch[:, None])
    allowed = allowed.astype(jnp.float32)
    return jnp.concatenate([allowed, allowed], axis=0)


def rounded_sum(*values):
    total = values[0].astype(jnp.float32)
    for value in values[1:]:
        total = total + value.astype(jnp.float32)
    return total.astype(jnp.bfloat16)


def pick(value, index, axis):
    return lax.dynamic_index_in_dim(value, index, axis, keepdims=False)


def core_step(term):
    y_count, x_count, cores = (lax.axis_size(axis) for axis in FSDP)
    core = lax.axis_index("core")
    rows = term.shape[0] // (y_count * x_count * cores)
    split = term.reshape(y_count, x_count, cores, rows, term.shape[1])
    return rounded_sum(pick(split, core, 2), shift_over(pick(split, 1 - core, 2), "core", 1))


def x_first_step(both):
    opposite = pick(both, (lax.axis_index("x") + 2) % 4, 1)
    half = opposite.shape[1] // 2
    return shift_over(opposite[:, :half], "x", 1), shift_over(opposite[:, half:], "x", -1)


def x_second_step(both, from_left, from_right):
    x = lax.axis_index("x")
    half = both.shape[2] // 2
    up, down = pick(both, (x + 1) % 4, 1), pick(both, (x + 3) % 4, 1)
    up = jnp.concatenate([rounded_sum(up[:, :half], from_left), up[:, half:]], axis=1)
    down = jnp.concatenate([down[:, :half], rounded_sum(down[:, half:], from_right)], axis=1)
    return rounded_sum(pick(both, x, 1), shift_over(up, "x", 1), shift_over(down, "x", -1))


def y_step(column):
    y = lax.axis_index("yl")
    return rounded_sum(pick(column, y, 0), shift_over(pick(column, 1 - y, 0), "yl", 1))


def sum_over_group(shard):
    count = lax.axis_size("pair") * lax.axis_size("tm")
    parts = shard.reshape(count, -1, 128)
    received = lax.all_to_all(parts, GROUP, split_axis=0, concat_axis=0, tiled=True)
    mine = jnp.sum(received.astype(jnp.float32), axis=0).astype(jnp.bfloat16)
    spread = jnp.broadcast_to(mine[None], parts.shape)
    whole = lax.all_to_all(spread, GROUP, split_axis=0, concat_axis=0, tiled=True)
    return whole.reshape(shard.shape)


def on_device(frames, frame_time, w_qkv, w_out, grad_out):
    inner = w_out.shape[0]
    width = frames.shape[-1]
    gathered = lax.all_gather(
        jnp.concatenate([w_qkv, w_out.T], axis=1), FSDP, axis=0, tiled=True
    )
    full_qkv = gathered[:, : 3 * inner]
    tokens = to_patch_owner(frames)
    grad_parts, steps = parts_to_patch_owners(grad_out)
    token_shape = tokens.shape
    senders, patches_each, frames_each = token_shape[:3]
    mask = attention_mask(frame_time, senders, frames_each)

    float_rows = tokens.reshape(-1, width).astype(jnp.float32)
    inv_rms = lax.rsqrt(jnp.mean(float_rows * float_rows, axis=-1, keepdims=True) + 1e-06)
    normed = (float_rows * inv_rms).astype(jnp.bfloat16)
    qkv = jnp.dot(normed, full_qkv, preferred_element_type=jnp.float32).astype(jnp.bfloat16)
    qkv = qkv.reshape(token_shape[:3] + (3 * inner,))
    mixed, weights = attention_forward(qkv, mask, inner)

    grad_tokens, d_mixed = project(grad_parts, steps, gathered, 3 * inner, inner)
    grad_rows = grad_tokens.reshape(-1, width)
    term_out = contract(grad_rows, mixed.reshape(-1, inner), 0, 0).astype(jnp.bfloat16)
    both_out = core_step(term_out)
    d_mixed = after(d_mixed, both_out)
    groups = patches_each // 2
    d_qkv = attention_backward(qkv, d_mixed, weights, None, 0, groups // 2)
    from_left, from_right = x_first_step(both_out)
    d_qkv = after(d_qkv, from_left, from_right)
    d_qkv = attention_backward(qkv, d_mixed, weights, d_qkv, groups // 2, groups - groups // 2)
    d_rows = d_qkv.reshape(-1, 3 * inner)

    shard_out = y_step(x_second_step(both_out, from_left, from_right))
    cut = 3 * inner // 2
    both_first, both_second = [
        core_step(contract(normed, part, 0, 0).astype(jnp.bfloat16))
        for part in (d_rows[:, :cut], d_rows[:, cut:])
    ]

    d_normed = contract(d_rows, full_qkv, 1, 1)
    scaled = float_rows * inv_rms
    inner_term = jnp.mean(d_normed * scaled, axis=-1, keepdims=True)
    grad_local = grad_rows.astype(jnp.float32) + inv_rms * (d_normed - scaled * inner_term)
    grad_local = grad_local.astype(jnp.bfloat16).reshape(token_shape)
    grad_frames = to_frame_owner(grad_local)

    shard_first = y_step(x_second_step(both_first, *x_first_step(both_first)))
    column = y_step(both_second)[None]
    column_parts = x_first_step(after(column, grad_local))
    shard_second = x_second_step(column, *column_parts)[0]
    shards = jnp.concatenate([shard_first, shard_second, shard_out], axis=1)
    summed = sum_over_group(after(shards, grad_frames)).astype(jnp.float32)
    summed_qkv, summed_out = summed[:, : 3 * inner], summed[:, 3 * inner :]
    tokens_all = frames.shape[0] * frames.shape[1] * frames.shape[2]
    for axis in GROUP + FSDP:
        tokens_all *= lax.axis_size(axis)
    grad_scale = 1.0 / math.sqrt(tokens_all)
    return (grad_frames, summed_qkv * grad_scale, summed_out.T * grad_scale)


def solution(mesh):
    pairs, times, shards = (mesh.shape[name] for name in ("pair", "tm", "fsdp"))
    cut = Mesh(
        mesh.devices.reshape(pairs, times, 2, shards // 4, 2), ("pair", "tm") + FSDP
    )
    tokens_spec = P("pair", "tm", FSDP, None)
    return jax.shard_map(
        on_device,
        mesh=cut,
        in_specs=(tokens_spec, P("pair", None), P(FSDP, None), P(None, FSDP), tokens_spec),
        out_specs=(tokens_spec, P(FSDP, None), P(None, FSDP)),
        check_vma=False,
    )
```

```python
import functools
import math

import jax
import jax.numpy as jnp
import numpy as np
from jax import lax
from jax.experimental import pallas as pl
from jax.experimental.pallas import tpu as pltpu
from jax.sharding import Mesh
from jax.sharding import PartitionSpec as P

HEAD_DIM = 64
FSDP = ("yl", "x", "core")
GROUP = ("pair", "tm")
MASKED = -1e30
VMEM_BYTES = 48 * 1024 * 1024


def low_half(rows):
    return lax.broadcasted_iota(jnp.int32, (rows, 2 * HEAD_DIM), 1) < HEAD_DIM


def stack_heads(pair_rows):
    first = low_half(pair_rows.shape[0])
    zero = jnp.zeros_like(pair_rows)
    return jnp.concatenate([jnp.where(first, pair_rows, zero), jnp.where(first, zero, pair_rows)], axis=0)


def merge_heads(stacked):
    rows = stacked.shape[0] // 2
    return jnp.where(low_half(rows), stacked[:rows], stacked[rows:])


def contract(left, right, left_dim, right_dim):
    return lax.dot_general(
        left, right, (((left_dim,), (right_dim,)), ((), ())), preferred_element_type=jnp.float32
    )


def forward_kernel(mask_ref, qkv_ref, mixed_ref, weights_ref):
    wide = 2 * HEAD_DIM
    inner = mixed_ref.shape[-1]
    rows = mask_ref.shape[1]
    allowed = mask_ref[...] > 0.5
    for pair in range(inner // wide):
        first = pair * wide
        queries = stack_heads(qkv_ref[..., first : first + wide].reshape(rows, wide))
        keys = qkv_ref[..., inner + first : inner + first + wide].reshape(rows, wide)
        values = qkv_ref[..., 2 * inner + first : 2 * inner + first + wide].reshape(rows, wide)
        scores = contract(queries, keys, 1, 1) * HEAD_DIM ** (-0.5)
        scores = jnp.where(allowed, scores, MASKED)
        exponent = jnp.exp(scores - jnp.max(scores, axis=-1, keepdims=True))
        weights = exponent / jnp.sum(exponent, axis=-1, keepdims=True)
        weights_ref[0, pair] = weights
        mixed = merge_heads(contract(weights.astype(jnp.bfloat16), values, 1, 0))
        mixed_ref[..., first : first + wide] = mixed.astype(jnp.bfloat16).reshape(
            mixed_ref.shape[:-1] + (wide,)
        )


def backward_kernel(qkv_ref, d_mixed_ref, weights_ref, d_qkv_ref):
    wide = 2 * HEAD_DIM
    inner = d_mixed_ref.shape[-1]
    rows = weights_ref.shape[-1]
    block = d_mixed_ref.shape[:-1] + (wide,)
    for pair in range(inner // wide):
        first = pair * wide
        queries = stack_heads(qkv_ref[..., first : first + wide].reshape(rows, wide))
        keys = qkv_ref[..., inner + first : inner + first + wide].reshape(rows, wide)
        values = qkv_ref[..., 2 * inner + first : 2 * inner + first + wide].reshape(rows, wide)
        d_heads = stack_heads(d_mixed_ref[..., first : first + wide].reshape(rows, wide))
        weights = weights_ref[0, pair]
        d_weights = contract(d_heads, values, 1, 1)
        centered = d_weights - jnp.sum(weights * d_weights, axis=-1, keepdims=True)
        d_scores = (weights * centered * HEAD_DIM ** (-0.5)).astype(jnp.bfloat16)
        d_query = merge_heads(contract(d_scores, keys, 1, 0))
        d_key = contract(d_scores, queries, 0, 0)
        d_value = contract(weights.astype(jnp.bfloat16), d_heads, 0, 0)
        for place, value in enumerate((d_query, d_key, d_value)):
            start = place * inner + first
            d_qkv_ref[..., start : start + wide] = value.astype(jnp.bfloat16).reshape(block)


def attention_forward(qkv, mask, inner):
    senders, patches, frames_each, triple = qkv.shape
    groups = patches // 2
    rows = senders * 2 * frames_each
    pairs = inner // (2 * HEAD_DIM)
    return pl.pallas_call(
        forward_kernel,
        grid=(groups,),
        in_specs=[
            pl.BlockSpec((2 * rows, rows), lambda g: (0, 0)),
            pl.BlockSpec((senders, 2, frames_each, triple), lambda g: (0, g, 0, 0)),
        ],
        out_specs=[
            pl.BlockSpec((senders, 2, frames_each, inner), lambda g: (0, g, 0, 0)),
            pl.BlockSpec((1, pairs, 2 * rows, rows), lambda g: (g, 0, 0, 0)),
        ],
        out_shape=[
            jax.ShapeDtypeStruct((senders, patches, frames_each, inner), jnp.bfloat16),
            jax.ShapeDtypeStruct((groups, pairs, 2 * rows, rows), jnp.float32),
        ],
        compiler_params=pltpu.CompilerParams(vmem_limit_bytes=VMEM_BYTES),
        cost_estimate=pl.CostEstimate(
            flops=groups * pairs * 2 * 2 * rows * rows * 256,
            bytes_accessed=8 * 1024 * 1024,
            transcendentals=groups * pairs * 2 * rows * rows,
        ),
    )(mask, qkv)


def attention_backward(qkv, d_mixed, weights):
    senders, patches, frames_each, inner = d_mixed.shape
    groups, pairs, double_rows, rows = weights.shape
    return pl.pallas_call(
        backward_kernel,
        grid=(groups,),
        in_specs=[
            pl.BlockSpec((senders, 2, frames_each, 3 * inner), lambda g: (0, g, 0, 0)),
            pl.BlockSpec((senders, 2, frames_each, inner), lambda g: (0, g, 0, 0)),
            pl.BlockSpec((1, pairs, double_rows, rows), lambda g: (g, 0, 0, 0)),
        ],
        out_specs=pl.BlockSpec((senders, 2, frames_each, 3 * inner), lambda g: (0, g, 0, 0)),
        out_shape=jax.ShapeDtypeStruct((senders, patches, frames_each, 3 * inner), jnp.bfloat16),
        compiler_params=pltpu.CompilerParams(vmem_limit_bytes=VMEM_BYTES),
        cost_estimate=pl.CostEstimate(
            flops=groups * pairs * 4 * 2 * rows * rows * 256,
            bytes_accessed=10 * 1024 * 1024,
            transcendentals=0,
        ),
    )(qkv, d_mixed, weights)


def shift_over(value, axis, step):
    count = lax.axis_size(axis)
    return lax.ppermute(value, axis, [(i, (i + step) % count) for i in range(count)])


def far_first(count):
    return sorted(range(1, count), key=lambda step: -min(step, count - step))


def split_kernel(me_ref, rows_ref, *part_refs):
    frames_each, owners, patches_each, width = rows_ref.shape
    count = frames_each * patches_each
    out_row = lax.broadcasted_iota(jnp.int32, (count, count), 0)
    in_row = lax.broadcasted_iota(jnp.int32, (count, count), 1)
    source = (out_row % frames_each) * patches_each + out_row // frames_each
    turn = (in_row == source).astype(jnp.bfloat16)
    for step, part_ref in enumerate(part_refs):
        part = rows_ref[:, lax.rem(me_ref[0] + step, owners)].reshape(count, width)
        turned = jnp.dot(turn, part, preferred_element_type=jnp.float32).astype(jnp.bfloat16)
        part_ref[...] = turned.reshape(part_ref.shape)


def join_kernel(steps, me_ref, *refs):
    owners = len(steps)
    part_refs = refs[:owners]
    rows_ref, normed_ref, sems = refs[owners:]
    copies = []
    for step, part_ref in zip(steps, part_refs):
        place = lax.rem(me_ref[0] + owners - step, owners)
        copies.append(pltpu.make_async_copy(part_ref, rows_ref.at[place], sems.at[step]))
    for copy in copies:
        copy.start()
    for copy in copies:
        copy.wait()
    for place in range(owners):
        rows = rows_ref[place].astype(jnp.float32)
        inv_rms = lax.rsqrt(jnp.mean(rows * rows, axis=-1, keepdims=True) + 1e-06)
        normed_ref[place] = (rows * inv_rms).astype(jnp.bfloat16)


def project_kernel(steps, me_ref, *refs):
    owners = len(steps)
    part_refs = refs[:owners]
    weight_ref, rows_ref, product_ref, sems = refs[owners:]
    width = rows_ref.shape[-1]

    @pl.when(pl.program_id(0) == 0)
    def _():
        copies = []
        for step, part_ref in zip(steps, part_refs):
            place = lax.rem(me_ref[0] + owners - step, owners)
            copies.append(pltpu.make_async_copy(part_ref, rows_ref.at[place], sems.at[step]))
        for copy in copies:
            copy.start()
        for copy in copies:
            copy.wait()

    product = jnp.dot(
        rows_ref[...].reshape(-1, width), weight_ref[...], preferred_element_type=jnp.float32
    )
    product_ref[...] = product.astype(jnp.bfloat16).reshape(product_ref.shape)


IN_SMEM = pl.BlockSpec(memory_space=pltpu.SMEM)
IN_VMEM = pl.BlockSpec(memory_space=pltpu.VMEM)
ANYWHERE = pl.BlockSpec(memory_space=pl.ANY)


def after(value, *others):
    return lax.optimization_barrier((value,) + others)[0]


def parts_to_patch_owners(block):
    frames_each, patches_here, width = block.shape[1:]
    owners = lax.axis_size("tm")
    part = jax.ShapeDtypeStruct((patches_here // owners, frames_each, width), block.dtype)
    parts = pl.pallas_call(
        split_kernel,
        in_specs=[IN_SMEM, IN_VMEM],
        out_specs=[IN_VMEM] * owners,
        out_shape=[part] * owners,
        compiler_params=pltpu.CompilerParams(vmem_limit_bytes=VMEM_BYTES),
        cost_estimate=pl.CostEstimate(flops=2 * 64 * block.size, bytes_accessed=4 * block.size, transcendentals=0),
    )(lax.axis_index("tm").reshape(1), block.reshape(frames_each, owners, patches_here // owners, width))
    steps = far_first(owners)
    return [parts[0]] + [shift_over(parts[step], "tm", step) for step in steps], (0, *steps)


def join_and_normalize(parts, steps):
    owners = len(parts)
    whole = jax.ShapeDtypeStruct((owners,) + parts[0].shape, jnp.bfloat16)
    return pl.pallas_call(
        functools.partial(join_kernel, steps),
        in_specs=[IN_SMEM] + [ANYWHERE] * owners,
        out_specs=[IN_VMEM, IN_VMEM],
        out_shape=[whole, whole],
        scratch_shapes=[pltpu.SemaphoreType.DMA((owners,))],
        compiler_params=pltpu.CompilerParams(vmem_limit_bytes=VMEM_BYTES),
        cost_estimate=pl.CostEstimate(flops=8 * whole.size, bytes_accessed=6 * whole.size, transcendentals=512),
    )(lax.axis_index("tm").reshape(1), *parts)


def project(parts, steps, gathered, first, columns):
    owners = len(parts)
    patches_each, frames_each, width = parts[0].shape
    token_shape = (owners, patches_each, frames_each)
    block = 256
    return pl.pallas_call(
        functools.partial(project_kernel, steps),
        grid=(columns // block,),
        in_specs=[IN_SMEM]
        + [ANYWHERE] * owners
        + [pl.BlockSpec((width, block), lambda j: (0, j + first // block))],
        out_specs=[
            pl.BlockSpec(token_shape + (width,), lambda j: (0, 0, 0, 0)),
            pl.BlockSpec(token_shape + (block,), lambda j: (0, 0, 0, j)),
        ],
        out_shape=[
            jax.ShapeDtypeStruct(token_shape + (width,), jnp.bfloat16),
            jax.ShapeDtypeStruct(token_shape + (columns,), jnp.bfloat16),
        ],
        scratch_shapes=[pltpu.SemaphoreType.DMA((owners,))],
        compiler_params=pltpu.CompilerParams(vmem_limit_bytes=VMEM_BYTES),
        cost_estimate=pl.CostEstimate(
            flops=2 * 512 * width * columns, bytes_accessed=2 * width * columns, transcendentals=0
        ),
    )(lax.axis_index("tm").reshape(1), *parts, gathered)


def to_frame_owner(block):
    owners, patches_each, frames_each, width = block.shape
    back = lax.all_to_all(block, "tm", split_axis=0, concat_axis=0, tiled=True)
    return back.transpose(2, 0, 1, 3).reshape(1, frames_each, owners * patches_each, width)


def attention_mask(frame_time, senders, frames_each):
    rows = np.arange(senders * 2 * frames_each)
    patch = (rows // frames_each) % 2
    frame = (rows // (2 * frames_each)) * frames_each + rows % frames_each
    times = frame_time[0][frame]
    allowed = (times[None, :] <= times[:, None]) & (patch[None, :] == patch[:, None])
    allowed = allowed.astype(jnp.float32)
    return jnp.concatenate([allowed, allowed], axis=0)


def rounded_sum(*values):
    total = values[0].astype(jnp.float32)
    for value in values[1:]:
        total = total + value.astype(jnp.float32)
    return total.astype(jnp.bfloat16)


def pick(value, index, axis):
    return lax.dynamic_index_in_dim(value, index, axis, keepdims=False)


def core_swap(term):
    y_count, x_count, cores = (lax.axis_size(axis) for axis in FSDP)
    core = lax.axis_index("core")
    rows = term.shape[0] // (y_count * x_count * cores)
    split = term.reshape(y_count, x_count, cores, rows, term.shape[1])
    return pick(split, core, 2), shift_over(pick(split, 1 - core, 2), "core", 1)


def x_first_step(both):
    opposite = pick(both, (lax.axis_index("x") + 2) % 4, 1)
    half = opposite.shape[1] // 2
    return shift_over(opposite[:, :half], "x", 1), shift_over(opposite[:, half:], "x", -1)


def x_second_parts(both, from_left, from_right):
    x = lax.axis_index("x")
    half = both.shape[2] // 2
    up, down = pick(both, (x + 1) % 4, 1), pick(both, (x + 3) % 4, 1)
    up = jnp.concatenate([rounded_sum(up[:, :half], from_left), up[:, half:]], axis=1)
    down = jnp.concatenate([down[:, :half], rounded_sum(down[:, half:], from_right)], axis=1)
    return up, down


def x_second_step(up, down):
    return shift_over(up, "x", 1), shift_over(down, "x", -1)


def x_own(both):
    return pick(both, lax.axis_index("x"), 1)


def y_swap(column):
    y = lax.axis_index("yl")
    return pick(column, y, 0), shift_over(pick(column, 1 - y, 0), "yl", 1)


def sum_over_group(shard):
    count = lax.axis_size("pair") * lax.axis_size("tm")
    parts = shard.reshape(count, -1, 128)
    received = lax.all_to_all(parts, GROUP, split_axis=0, concat_axis=0, tiled=True)
    mine = jnp.sum(received.astype(jnp.float32), axis=0).astype(jnp.bfloat16)
    spread = jnp.broadcast_to(mine[None], parts.shape)
    whole = lax.all_to_all(spread, GROUP, split_axis=0, concat_axis=0, tiled=True)
    return whole.reshape(shard.shape)


def on_device(frames, frame_time, w_qkv, w_out, grad_out):
    inner = w_out.shape[0]
    width = frames.shape[-1]
    gathered = lax.all_gather(
        jnp.concatenate([w_qkv, w_out.T], axis=1), FSDP, axis=0, tiled=True
    )
    full_qkv = gathered[:, : 3 * inner]
    token_parts, steps = parts_to_patch_owners(frames)
    grad_parts, steps = parts_to_patch_owners(grad_out)
    tokens, normed = join_and_normalize(token_parts, steps)
    token_shape = tokens.shape
    senders, patches_each, frames_each = token_shape[:3]
    mask = attention_mask(frame_time, senders, frames_each)

    float_rows = tokens.reshape(-1, width).astype(jnp.float32)
    inv_rms = lax.rsqrt(jnp.mean(float_rows * float_rows, axis=-1, keepdims=True) + 1e-06)
    normed = normed.reshape(-1, width)
    normed = after(normed, inv_rms)
    qkv = jnp.dot(normed, full_qkv, preferred_element_type=jnp.float32).astype(jnp.bfloat16)
    qkv = qkv.reshape(token_shape[:3] + (3 * inner,))
    mixed, weights = attention_forward(qkv, mask, inner)

    grad_tokens, d_mixed = project(grad_parts, steps, gathered, 3 * inner, inner)
    grad_rows = grad_tokens.reshape(-1, width)
    d_qkv = attention_backward(qkv, d_mixed, weights)
    d_rows = d_qkv.reshape(-1, 3 * inner)

    cut = 3 * inner // 2
    first_term = contract(normed, d_rows[:, :cut], 0, 0).astype(jnp.bfloat16)
    first_keep, first_swapped = core_swap(first_term)
    second_term = contract(normed, after(d_rows, first_term)[:, cut:], 0, 0).astype(jnp.bfloat16)
    second_keep, second_swapped = core_swap(second_term)
    both_first = rounded_sum(first_keep, after(first_swapped, second_term))
    first_left, first_right = x_first_step(both_first)
    both_second = rounded_sum(second_keep, after(second_swapped, both_first))
    second_own, second_moved = y_swap(both_second)
    mixed_rows = after(mixed.reshape(-1, inner), both_second)
    term_out = contract(grad_rows, mixed_rows, 0, 0).astype(jnp.bfloat16)
    out_keep, out_swapped = core_swap(term_out)

    d_rows, grad_rows = lax.optimization_barrier((d_rows, grad_rows, term_out))[:2]
    d_normed = contract(d_rows, full_qkv, 1, 1)
    scaled = float_rows * inv_rms
    inner_term = jnp.mean(d_normed * scaled, axis=-1, keepdims=True)
    grad_local = grad_rows.astype(jnp.float32) + inv_rms * (d_normed - scaled * inner_term)
    grad_local = grad_local.astype(jnp.bfloat16).reshape(token_shape)
    grad_frames = to_frame_owner(grad_local)

    first_left, first_right, out_swapped = lax.optimization_barrier(
        (first_left, first_right, out_swapped, grad_local)
    )[:3]
    up, down = x_second_parts(both_first, first_left, first_right)
    first_moved = x_second_step(up, down)
    out_swapped, second_moved = lax.optimization_barrier((out_swapped, second_moved, up, down))[:2]
    both_out = rounded_sum(out_keep, out_swapped)
    out_parts = x_second_parts(both_out, *x_first_step(both_out))
    shard_out = rounded_sum(*y_swap(rounded_sum(x_own(both_out), *x_second_step(*out_parts))))

    column = rounded_sum(second_own, second_moved)[None]
    column_moved = x_second_step(*x_second_parts(column, *x_first_step(column)))
    shard_first = rounded_sum(*y_swap(rounded_sum(x_own(both_first), *first_moved)))
    shard_second = rounded_sum(x_own(column), *column_moved)[0]
    shards = jnp.concatenate([shard_first, shard_second, shard_out], axis=1)
    summed = sum_over_group(after(shards, grad_frames)).astype(jnp.float32)
    summed_qkv, summed_out = summed[:, : 3 * inner], summed[:, 3 * inner :]
    tokens_all = frames.shape[0] * frames.shape[1] * frames.shape[2]
    for axis in GROUP + FSDP:
        tokens_all *= lax.axis_size(axis)
    grad_scale = 1.0 / math.sqrt(tokens_all)
    return (grad_frames, summed_qkv * grad_scale, summed_out.T * grad_scale)


def solution(mesh):
    pairs, times, shards = (mesh.shape[name] for name in ("pair", "tm", "fsdp"))
    cut = Mesh(
        mesh.devices.reshape(pairs, times, 2, shards // 4, 2), ("pair", "tm") + FSDP
    )
    tokens_spec = P("pair", "tm", FSDP, None)
    return jax.shard_map(
        on_device,
        mesh=cut,
        in_specs=(tokens_spec, P("pair", None), P(FSDP, None), P(None, FSDP), tokens_spec),
        out_specs=(tokens_spec, P(FSDP, None), P(None, FSDP)),
        check_vma=False,
    )
```

```python
import functools
import math

import jax
import jax.numpy as jnp
import numpy as np
from jax import lax
from jax.experimental import pallas as pl
from jax.experimental.pallas import tpu as pltpu
from jax.sharding import Mesh
from jax.sharding import PartitionSpec as P

HEAD_DIM = 64
FSDP = ("yl", "x", "core")
GROUP = ("pair", "tm")
MASKED = -1e30
VMEM_BYTES = 48 * 1024 * 1024


def low_half(rows):
    return lax.broadcasted_iota(jnp.int32, (rows, 2 * HEAD_DIM), 1) < HEAD_DIM


def stack_heads(pair_rows):
    first = low_half(pair_rows.shape[0])
    zero = jnp.zeros_like(pair_rows)
    return jnp.concatenate([jnp.where(first, pair_rows, zero), jnp.where(first, zero, pair_rows)], axis=0)


def merge_heads(stacked):
    rows = stacked.shape[0] // 2
    return jnp.where(low_half(rows), stacked[:rows], stacked[rows:])


def contract(left, right, left_dim, right_dim):
    return lax.dot_general(
        left, right, (((left_dim,), (right_dim,)), ((), ())), preferred_element_type=jnp.float32
    )


def forward_kernel(mask_ref, qkv_ref, mixed_ref, weights_ref):
    wide = 2 * HEAD_DIM
    inner = mixed_ref.shape[-1]
    rows = mask_ref.shape[1]
    allowed = mask_ref[...] > 0.5
    for pair in range(inner // wide):
        first = pair * wide
        queries = stack_heads(qkv_ref[..., first : first + wide].reshape(rows, wide))
        keys = qkv_ref[..., inner + first : inner + first + wide].reshape(rows, wide)
        values = qkv_ref[..., 2 * inner + first : 2 * inner + first + wide].reshape(rows, wide)
        scores = contract(queries, keys, 1, 1) * HEAD_DIM ** (-0.5)
        scores = jnp.where(allowed, scores, MASKED)
        exponent = jnp.exp(scores - jnp.max(scores, axis=-1, keepdims=True))
        weights = exponent / jnp.sum(exponent, axis=-1, keepdims=True)
        weights_ref[0, pair] = weights
        mixed = merge_heads(contract(weights.astype(jnp.bfloat16), values, 1, 0))
        mixed_ref[..., first : first + wide] = mixed.astype(jnp.bfloat16).reshape(
            mixed_ref.shape[:-1] + (wide,)
        )


def backward_kernel(qkv_ref, d_mixed_ref, weights_ref, d_qkv_ref):
    wide = 2 * HEAD_DIM
    inner = d_mixed_ref.shape[-1]
    rows = weights_ref.shape[-1]
    block = d_mixed_ref.shape[:-1] + (wide,)
    for pair in range(inner // wide):
        first = pair * wide
        queries = stack_heads(qkv_ref[..., first : first + wide].reshape(rows, wide))
        keys = qkv_ref[..., inner + first : inner + first + wide].reshape(rows, wide)
        values = qkv_ref[..., 2 * inner + first : 2 * inner + first + wide].reshape(rows, wide)
        d_heads = stack_heads(d_mixed_ref[..., first : first + wide].reshape(rows, wide))
        weights = weights_ref[0, pair]
        d_weights = contract(d_heads, values, 1, 1)
        centered = d_weights - jnp.sum(weights * d_weights, axis=-1, keepdims=True)
        d_scores = (weights * centered * HEAD_DIM ** (-0.5)).astype(jnp.bfloat16)
        d_query = merge_heads(contract(d_scores, keys, 1, 0))
        d_key = contract(d_scores, queries, 0, 0)
        d_value = contract(weights.astype(jnp.bfloat16), d_heads, 0, 0)
        for place, value in enumerate((d_query, d_key, d_value)):
            start = place * inner + first
            d_qkv_ref[..., start : start + wide] = value.astype(jnp.bfloat16).reshape(block)


def attention_forward(qkv, mask, inner):
    senders, patches, frames_each, triple = qkv.shape
    groups = patches // 2
    rows = senders * 2 * frames_each
    pairs = inner // (2 * HEAD_DIM)
    return pl.pallas_call(
        forward_kernel,
        grid=(groups,),
        in_specs=[
            pl.BlockSpec((2 * rows, rows), lambda g: (0, 0)),
            pl.BlockSpec((senders, 2, frames_each, triple), lambda g: (0, g, 0, 0)),
        ],
        out_specs=[
            pl.BlockSpec((senders, 2, frames_each, inner), lambda g: (0, g, 0, 0)),
            pl.BlockSpec((1, pairs, 2 * rows, rows), lambda g: (g, 0, 0, 0)),
        ],
        out_shape=[
            jax.ShapeDtypeStruct((senders, patches, frames_each, inner), jnp.bfloat16),
            jax.ShapeDtypeStruct((groups, pairs, 2 * rows, rows), jnp.float32),
        ],
        compiler_params=pltpu.CompilerParams(vmem_limit_bytes=VMEM_BYTES),
        cost_estimate=pl.CostEstimate(
            flops=groups * pairs * 2 * 2 * rows * rows * 256,
            bytes_accessed=8 * 1024 * 1024,
            transcendentals=groups * pairs * 2 * rows * rows,
        ),
    )(mask, qkv)


def attention_backward(qkv, d_mixed, weights):
    senders, patches, frames_each, inner = d_mixed.shape
    groups, pairs, double_rows, rows = weights.shape
    return pl.pallas_call(
        backward_kernel,
        grid=(groups,),
        in_specs=[
            pl.BlockSpec((senders, 2, frames_each, 3 * inner), lambda g: (0, g, 0, 0)),
            pl.BlockSpec((senders, 2, frames_each, inner), lambda g: (0, g, 0, 0)),
            pl.BlockSpec((1, pairs, double_rows, rows), lambda g: (g, 0, 0, 0)),
        ],
        out_specs=pl.BlockSpec((senders, 2, frames_each, 3 * inner), lambda g: (0, g, 0, 0)),
        out_shape=jax.ShapeDtypeStruct((senders, patches, frames_each, 3 * inner), jnp.bfloat16),
        compiler_params=pltpu.CompilerParams(vmem_limit_bytes=VMEM_BYTES),
        cost_estimate=pl.CostEstimate(
            flops=groups * pairs * 4 * 2 * rows * rows * 256,
            bytes_accessed=10 * 1024 * 1024,
            transcendentals=0,
        ),
    )(qkv, d_mixed, weights)


def shift_over(value, axis, step):
    count = lax.axis_size(axis)
    return lax.ppermute(value, axis, [(i, (i + step) % count) for i in range(count)])


def far_first(count):
    return sorted(range(1, count), key=lambda step: -min(step, count - step))


def split_kernel(me_ref, rows_ref, *part_refs):
    frames_each, owners, patches_each, width = rows_ref.shape
    count = frames_each * patches_each
    out_row = lax.broadcasted_iota(jnp.int32, (count, count), 0)
    in_row = lax.broadcasted_iota(jnp.int32, (count, count), 1)
    source = (out_row % frames_each) * patches_each + out_row // frames_each
    turn = (in_row == source).astype(jnp.bfloat16)
    for step, part_ref in enumerate(part_refs):
        part = rows_ref[:, lax.rem(me_ref[0] + step, owners)].reshape(count, width)
        turned = jnp.dot(turn, part, preferred_element_type=jnp.float32).astype(jnp.bfloat16)
        part_ref[...] = turned.reshape(part_ref.shape)


def join_kernel(steps, me_ref, *refs):
    owners = len(steps)
    part_refs = refs[:owners]
    rows_ref, normed_ref, sems = refs[owners:]
    copies = []
    for step, part_ref in zip(steps, part_refs):
        place = lax.rem(me_ref[0] + owners - step, owners)
        copies.append(pltpu.make_async_copy(part_ref, rows_ref.at[place], sems.at[step]))
    for copy in copies:
        copy.start()
    for copy in copies:
        copy.wait()
    for place in range(owners):
        rows = rows_ref[place].astype(jnp.float32)
        inv_rms = lax.rsqrt(jnp.mean(rows * rows, axis=-1, keepdims=True) + 1e-06)
        normed_ref[place] = (rows * inv_rms).astype(jnp.bfloat16)


def project_kernel(steps, me_ref, *refs):
    owners = len(steps)
    part_refs = refs[:owners]
    weight_ref, rows_ref, product_ref, sems = refs[owners:]
    width = rows_ref.shape[-1]

    @pl.when(pl.program_id(0) == 0)
    def _():
        copies = []
        for step, part_ref in zip(steps, part_refs):
            place = lax.rem(me_ref[0] + owners - step, owners)
            copies.append(pltpu.make_async_copy(part_ref, rows_ref.at[place], sems.at[step]))
        for copy in copies:
            copy.start()
        for copy in copies:
            copy.wait()

    product = jnp.dot(
        rows_ref[...].reshape(-1, width), weight_ref[...], preferred_element_type=jnp.float32
    )
    product_ref[...] = product.astype(jnp.bfloat16).reshape(product_ref.shape)


IN_SMEM = pl.BlockSpec(memory_space=pltpu.SMEM)
IN_VMEM = pl.BlockSpec(memory_space=pltpu.VMEM)
ANYWHERE = pl.BlockSpec(memory_space=pl.ANY)


def after(value, *others):
    return lax.optimization_barrier((value,) + others)[0]


def parts_to_patch_owners(block):
    frames_each, patches_here, width = block.shape[1:]
    owners = lax.axis_size("tm")
    part = jax.ShapeDtypeStruct((patches_here // owners, frames_each, width), block.dtype)
    parts = pl.pallas_call(
        split_kernel,
        in_specs=[IN_SMEM, IN_VMEM],
        out_specs=[IN_VMEM] * owners,
        out_shape=[part] * owners,
        compiler_params=pltpu.CompilerParams(vmem_limit_bytes=VMEM_BYTES),
        cost_estimate=pl.CostEstimate(flops=2 * 64 * block.size, bytes_accessed=4 * block.size, transcendentals=0),
    )(lax.axis_index("tm").reshape(1), block.reshape(frames_each, owners, patches_here // owners, width))
    steps = far_first(owners)
    return [parts[0]] + [shift_over(parts[step], "tm", step) for step in steps], (0, *steps)


def join_and_normalize(parts, steps):
    owners = len(parts)
    whole = jax.ShapeDtypeStruct((owners,) + parts[0].shape, jnp.bfloat16)
    return pl.pallas_call(
        functools.partial(join_kernel, steps),
        in_specs=[IN_SMEM] + [ANYWHERE] * owners,
        out_specs=[IN_VMEM, IN_VMEM],
        out_shape=[whole, whole],
        scratch_shapes=[pltpu.SemaphoreType.DMA((owners,))],
        compiler_params=pltpu.CompilerParams(vmem_limit_bytes=VMEM_BYTES),
        cost_estimate=pl.CostEstimate(flops=8 * whole.size, bytes_accessed=6 * whole.size, transcendentals=512),
    )(lax.axis_index("tm").reshape(1), *parts)


def project(parts, steps, gathered, first, columns):
    owners = len(parts)
    patches_each, frames_each, width = parts[0].shape
    token_shape = (owners, patches_each, frames_each)
    block = 768
    return pl.pallas_call(
        functools.partial(project_kernel, steps),
        grid=(columns // block,),
        in_specs=[IN_SMEM]
        + [ANYWHERE] * owners
        + [pl.BlockSpec((width, block), lambda j: (0, j + first // block))],
        out_specs=[
            pl.BlockSpec(token_shape + (width,), lambda j: (0, 0, 0, 0)),
            pl.BlockSpec(token_shape + (block,), lambda j: (0, 0, 0, j)),
        ],
        out_shape=[
            jax.ShapeDtypeStruct(token_shape + (width,), jnp.bfloat16),
            jax.ShapeDtypeStruct(token_shape + (columns,), jnp.bfloat16),
        ],
        scratch_shapes=[pltpu.SemaphoreType.DMA((owners,))],
        compiler_params=pltpu.CompilerParams(vmem_limit_bytes=VMEM_BYTES),
        cost_estimate=pl.CostEstimate(
            flops=2 * 512 * width * columns, bytes_accessed=2 * width * columns, transcendentals=0
        ),
    )(lax.axis_index("tm").reshape(1), *parts, gathered)


def in_frames(back):
    owners, patches_each, frames_each, width = back.shape
    return back.transpose(2, 0, 1, 3).reshape(1, frames_each, owners * patches_each, width)


def attention_mask(frame_time, senders, frames_each):
    rows = np.arange(senders * 2 * frames_each)
    patch = (rows // frames_each) % 2
    frame = (rows // (2 * frames_each)) * frames_each + rows % frames_each
    times = frame_time[0][frame]
    allowed = (times[None, :] <= times[:, None]) & (patch[None, :] == patch[:, None])
    allowed = allowed.astype(jnp.float32)
    return jnp.concatenate([allowed, allowed], axis=0)


def rounded_sum(*values):
    total = values[0].astype(jnp.float32)
    for value in values[1:]:
        total = total + value.astype(jnp.float32)
    return total.astype(jnp.bfloat16)


def pick(value, index, axis):
    return lax.dynamic_index_in_dim(value, index, axis, keepdims=False)


def core_swap(term):
    y_count, x_count, cores = (lax.axis_size(axis) for axis in FSDP)
    core = lax.axis_index("core")
    rows = term.shape[0] // (y_count * x_count * cores)
    split = term.reshape(y_count, x_count, cores, rows, term.shape[1])
    return pick(split, core, 2), shift_over(pick(split, 1 - core, 2), "core", 1)


def x_first_step(both):
    opposite = pick(both, (lax.axis_index("x") + 2) % 4, 1)
    half = opposite.shape[1] // 2
    return shift_over(opposite[:, :half], "x", 1), shift_over(opposite[:, half:], "x", -1)


def x_second_parts(both, from_left, from_right):
    x = lax.axis_index("x")
    half = both.shape[2] // 2
    up, down = pick(both, (x + 1) % 4, 1), pick(both, (x + 3) % 4, 1)
    up = jnp.concatenate([rounded_sum(up[:, :half], from_left), up[:, half:]], axis=1)
    down = jnp.concatenate([down[:, :half], rounded_sum(down[:, half:], from_right)], axis=1)
    return up, down


def x_second_step(up, down):
    return shift_over(up, "x", 1), shift_over(down, "x", -1)


def x_own(both):
    return pick(both, lax.axis_index("x"), 1)


def y_swap(column):
    y = lax.axis_index("yl")
    return pick(column, y, 0), shift_over(pick(column, 1 - y, 0), "yl", 1)


def sum_part_over_group(shard):
    count = lax.axis_size("pair") * lax.axis_size("tm")
    parts = shard.reshape(count, -1, 128)
    received = lax.all_to_all(parts, GROUP, split_axis=0, concat_axis=0, tiled=True)
    return jnp.sum(received.astype(jnp.float32), axis=0).astype(jnp.bfloat16)


def spread_over_group(part):
    count = lax.axis_size("pair") * lax.axis_size("tm")
    spread = jnp.broadcast_to(part[None], (count,) + part.shape)
    return lax.all_to_all(spread, GROUP, split_axis=0, concat_axis=0, tiled=True)


def on_device(frames, frame_time, w_qkv, w_out, grad_out):
    inner = w_out.shape[0]
    width = frames.shape[-1]
    gathered = lax.all_gather(
        jnp.concatenate([w_qkv, w_out.T], axis=1), FSDP, axis=0, tiled=True
    )
    full_qkv = gathered[:, : 3 * inner]
    token_parts, steps = parts_to_patch_owners(frames)
    grad_parts, steps = parts_to_patch_owners(grad_out)
    tokens, normed = join_and_normalize(token_parts, steps)
    token_shape = tokens.shape
    senders, patches_each, frames_each = token_shape[:3]
    mask = attention_mask(frame_time, senders, frames_each)

    float_rows = tokens.reshape(-1, width).astype(jnp.float32)
    inv_rms = lax.rsqrt(jnp.mean(float_rows * float_rows, axis=-1, keepdims=True) + 1e-06)
    normed = normed.reshape(-1, width)
    normed = after(normed, inv_rms)
    qkv = jnp.dot(normed, full_qkv, preferred_element_type=jnp.float32).astype(jnp.bfloat16)
    qkv = qkv.reshape(token_shape[:3] + (3 * inner,))
    mixed, weights = attention_forward(qkv, mask, inner)

    grad_tokens, d_mixed = project(grad_parts, steps, gathered, 3 * inner, inner)
    grad_rows = grad_tokens.reshape(-1, width)
    d_qkv = attention_backward(qkv, d_mixed, weights)
    d_rows = d_qkv.reshape(-1, 3 * inner)

    cut = 3 * inner // 2
    first_term = contract(normed, d_rows[:, :cut], 0, 0).astype(jnp.bfloat16)
    first_keep, first_swapped = core_swap(first_term)
    second_term = contract(normed, after(d_rows, first_term)[:, cut:], 0, 0).astype(jnp.bfloat16)
    second_keep, second_swapped = core_swap(second_term)
    both_first = rounded_sum(first_keep, after(first_swapped, second_term))
    first_left, first_right = x_first_step(both_first)
    both_second = rounded_sum(second_keep, after(second_swapped, both_first))
    second_own, second_moved = y_swap(both_second)
    mixed_rows = after(mixed.reshape(-1, inner), both_second)
    term_out = contract(grad_rows, mixed_rows, 0, 0).astype(jnp.bfloat16)
    out_keep, out_swapped = core_swap(term_out)

    d_rows, grad_rows = lax.optimization_barrier((d_rows, grad_rows, term_out))[:2]
    d_normed = contract(d_rows, full_qkv, 1, 1)
    scaled = float_rows * inv_rms
    inner_term = jnp.mean(d_normed * scaled, axis=-1, keepdims=True)
    grad_local = grad_rows.astype(jnp.float32) + inv_rms * (d_normed - scaled * inner_term)
    grad_local = grad_local.astype(jnp.bfloat16).reshape(token_shape)
    grad_back = lax.all_to_all(grad_local, "tm", split_axis=0, concat_axis=0, tiled=True)

    first_left, first_right, out_swapped = lax.optimization_barrier(
        (first_left, first_right, out_swapped, grad_local)
    )[:3]
    up, down = x_second_parts(both_first, first_left, first_right)
    first_moved = x_second_step(up, down)
    out_swapped, second_moved = lax.optimization_barrier((out_swapped, second_moved, up, down))[:2]
    both_out = rounded_sum(out_keep, out_swapped)
    out_parts = x_second_parts(both_out, *x_first_step(both_out))
    shard_out = rounded_sum(*y_swap(rounded_sum(x_own(both_out), *x_second_step(*out_parts))))

    column = rounded_sum(second_own, second_moved)[None]
    column_moved = x_second_step(*x_second_parts(column, *x_first_step(column)))
    shard_first = rounded_sum(*y_swap(rounded_sum(x_own(both_first), *first_moved)))
    shard_second = rounded_sum(x_own(column), *column_moved)[0]
    shards = jnp.concatenate([shard_first, shard_second, shard_out], axis=1)
    part = sum_part_over_group(after(shards, grad_back))
    grad_frames = in_frames(after(grad_back, part))
    summed = spread_over_group(part).reshape(shards.shape).astype(jnp.float32)
    summed_qkv, summed_out = summed[:, : 3 * inner], summed[:, 3 * inner :]
    tokens_all = frames.shape[0] * frames.shape[1] * frames.shape[2]
    for axis in GROUP + FSDP:
        tokens_all *= lax.axis_size(axis)
    grad_scale = 1.0 / math.sqrt(tokens_all)
    return (grad_frames, summed_qkv * grad_scale, summed_out.T * grad_scale)


def solution(mesh):
    pairs, times, shards = (mesh.shape[name] for name in ("pair", "tm", "fsdp"))
    cut = Mesh(
        mesh.devices.reshape(pairs, times, 2, shards // 4, 2), ("pair", "tm") + FSDP
    )
    tokens_spec = P("pair", "tm", FSDP, None)
    return jax.shard_map(
        on_device,
        mesh=cut,
        in_specs=(tokens_spec, P("pair", None), P(FSDP, None), P(None, FSDP), tokens_spec),
        out_specs=(tokens_spec, P(FSDP, None), P(None, FSDP)),
        check_vma=False,
    )
```

```python
import functools
import math

import jax
import jax.numpy as jnp
import numpy as np
from jax import lax
from jax.experimental import pallas as pl
from jax.experimental.pallas import tpu as pltpu
from jax.sharding import Mesh
from jax.sharding import PartitionSpec as P

HEAD_DIM = 64
FSDP = ("yl", "x", "core")
GROUP = ("pair", "tm")
MASKED = -1e30
VMEM_BYTES = 48 * 1024 * 1024


def low_half(rows):
    return lax.broadcasted_iota(jnp.int32, (rows, 2 * HEAD_DIM), 1) < HEAD_DIM


def stack_heads(pair_rows):
    first = low_half(pair_rows.shape[0])
    zero = jnp.zeros_like(pair_rows)
    return jnp.concatenate([jnp.where(first, pair_rows, zero), jnp.where(first, zero, pair_rows)], axis=0)


def merge_heads(stacked):
    rows = stacked.shape[0] // 2
    return jnp.where(low_half(rows), stacked[:rows], stacked[rows:])


def contract(left, right, left_dim, right_dim):
    return lax.dot_general(
        left, right, (((left_dim,), (right_dim,)), ((), ())), preferred_element_type=jnp.float32
    )


def forward_kernel(mask_ref, qkv_ref, mixed_ref, weights_ref):
    wide = 2 * HEAD_DIM
    inner = mixed_ref.shape[-1]
    rows = mask_ref.shape[1]
    allowed = mask_ref[...] > 0.5
    for pair in range(inner // wide):
        first = pair * wide
        queries = stack_heads(qkv_ref[..., first : first + wide].reshape(rows, wide))
        keys = qkv_ref[..., inner + first : inner + first + wide].reshape(rows, wide)
        values = qkv_ref[..., 2 * inner + first : 2 * inner + first + wide].reshape(rows, wide)
        scores = contract(queries, keys, 1, 1) * HEAD_DIM ** (-0.5)
        scores = jnp.where(allowed, scores, MASKED)
        exponent = jnp.exp(scores - jnp.max(scores, axis=-1, keepdims=True))
        weights = exponent / jnp.sum(exponent, axis=-1, keepdims=True)
        weights_ref[0, pair] = weights
        mixed = merge_heads(contract(weights.astype(jnp.bfloat16), values, 1, 0))
        mixed_ref[..., first : first + wide] = mixed.astype(jnp.bfloat16).reshape(
            mixed_ref.shape[:-1] + (wide,)
        )


def backward_kernel(qkv_ref, d_mixed_ref, weights_ref, d_qkv_ref):
    wide = 2 * HEAD_DIM
    inner = d_mixed_ref.shape[-1]
    rows = weights_ref.shape[-1]
    block = d_mixed_ref.shape[:-1] + (wide,)

    def load(pair):
        first = pair * wide
        values = qkv_ref[..., 2 * inner + first : 2 * inner + first + wide].reshape(rows, wide)
        d_heads = stack_heads(d_mixed_ref[..., first : first + wide].reshape(rows, wide))
        return d_heads, contract(d_heads, values, 1, 1)

    pairs = inner // wide
    ahead = load(0)
    for pair in range(pairs):
        first = pair * wide
        d_heads, d_weights = ahead
        if pair + 1 < pairs:
            ahead = load(pair + 1)
        queries = stack_heads(qkv_ref[..., first : first + wide].reshape(rows, wide))
        keys = qkv_ref[..., inner + first : inner + first + wide].reshape(rows, wide)
        weights = weights_ref[0, pair]
        d_value = contract(weights.astype(jnp.bfloat16), d_heads, 0, 0)
        centered = d_weights - jnp.sum(weights * d_weights, axis=-1, keepdims=True)
        d_scores = (weights * centered * HEAD_DIM ** (-0.5)).astype(jnp.bfloat16)
        d_query = merge_heads(contract(d_scores, keys, 1, 0))
        d_key = contract(d_scores, queries, 0, 0)
        for place, value in enumerate((d_query, d_key, d_value)):
            start = place * inner + first
            d_qkv_ref[..., start : start + wide] = value.astype(jnp.bfloat16).reshape(block)


def attention_forward(qkv, mask, inner):
    senders, patches, frames_each, triple = qkv.shape
    groups = patches // 2
    rows = senders * 2 * frames_each
    pairs = inner // (2 * HEAD_DIM)
    return pl.pallas_call(
        forward_kernel,
        grid=(groups,),
        in_specs=[
            pl.BlockSpec((2 * rows, rows), lambda g: (0, 0)),
            pl.BlockSpec((senders, 2, frames_each, triple), lambda g: (0, g, 0, 0)),
        ],
        out_specs=[
            pl.BlockSpec((senders, 2, frames_each, inner), lambda g: (0, g, 0, 0)),
            pl.BlockSpec((1, pairs, 2 * rows, rows), lambda g: (g, 0, 0, 0)),
        ],
        out_shape=[
            jax.ShapeDtypeStruct((senders, patches, frames_each, inner), jnp.bfloat16),
            jax.ShapeDtypeStruct((groups, pairs, 2 * rows, rows), jnp.float32),
        ],
        compiler_params=pltpu.CompilerParams(vmem_limit_bytes=VMEM_BYTES),
        cost_estimate=pl.CostEstimate(
            flops=groups * pairs * 2 * 2 * rows * rows * 256,
            bytes_accessed=8 * 1024 * 1024,
            transcendentals=groups * pairs * 2 * rows * rows,
        ),
    )(mask, qkv)


def attention_backward(qkv, d_mixed, weights):
    senders, patches, frames_each, inner = d_mixed.shape
    groups, pairs, double_rows, rows = weights.shape
    return pl.pallas_call(
        backward_kernel,
        grid=(groups,),
        in_specs=[
            pl.BlockSpec((senders, 2, frames_each, 3 * inner), lambda g: (0, g, 0, 0)),
            pl.BlockSpec((senders, 2, frames_each, inner), lambda g: (0, g, 0, 0)),
            pl.BlockSpec((1, pairs, double_rows, rows), lambda g: (g, 0, 0, 0)),
        ],
        out_specs=pl.BlockSpec((senders, 2, frames_each, 3 * inner), lambda g: (0, g, 0, 0)),
        out_shape=jax.ShapeDtypeStruct((senders, patches, frames_each, 3 * inner), jnp.bfloat16),
        compiler_params=pltpu.CompilerParams(vmem_limit_bytes=VMEM_BYTES),
        cost_estimate=pl.CostEstimate(
            flops=groups * pairs * 4 * 2 * rows * rows * 256,
            bytes_accessed=10 * 1024 * 1024,
            transcendentals=0,
        ),
    )(qkv, d_mixed, weights)


def shift_over(value, axis, step):
    count = lax.axis_size(axis)
    return lax.ppermute(value, axis, [(i, (i + step) % count) for i in range(count)])


def far_first(count):
    return sorted(range(1, count), key=lambda step: -min(step, count - step))


def split_kernel(me_ref, rows_ref, *part_refs):
    frames_each, owners, patches_each, width = rows_ref.shape
    count = frames_each * patches_each
    out_row = lax.broadcasted_iota(jnp.int32, (count, count), 0)
    in_row = lax.broadcasted_iota(jnp.int32, (count, count), 1)
    source = (out_row % frames_each) * patches_each + out_row // frames_each
    turn = (in_row == source).astype(jnp.bfloat16)
    for step, part_ref in enumerate(part_refs):
        part = rows_ref[:, lax.rem(me_ref[0] + step, owners)].reshape(count, width)
        turned = jnp.dot(turn, part, preferred_element_type=jnp.float32).astype(jnp.bfloat16)
        part_ref[...] = turned.reshape(part_ref.shape)


def join_kernel(steps, me_ref, *refs):
    owners = len(steps)
    part_refs = refs[:owners]
    rows_ref, normed_ref, sems = refs[owners:]
    copies = []
    for step, part_ref in zip(steps, part_refs):
        place = lax.rem(me_ref[0] + owners - step, owners)
        copies.append(pltpu.make_async_copy(part_ref, rows_ref.at[place], sems.at[step]))
    for copy in copies:
        copy.start()
    for copy in copies:
        copy.wait()
    for place in range(owners):
        rows = rows_ref[place].astype(jnp.float32)
        inv_rms = lax.rsqrt(jnp.mean(rows * rows, axis=-1, keepdims=True) + 1e-06)
        normed_ref[place] = (rows * inv_rms).astype(jnp.bfloat16)


def project_kernel(steps, me_ref, *refs):
    owners = len(steps)
    part_refs = refs[:owners]
    weight_ref, rows_ref, product_ref, sems = refs[owners:]
    width = rows_ref.shape[-1]

    @pl.when(pl.program_id(0) == 0)
    def _():
        copies = []
        for step, part_ref in zip(steps, part_refs):
            place = lax.rem(me_ref[0] + owners - step, owners)
            copies.append(pltpu.make_async_copy(part_ref, rows_ref.at[place], sems.at[step]))
        for copy in copies:
            copy.start()
        for copy in copies:
            copy.wait()

    product = jnp.dot(
        rows_ref[...].reshape(-1, width), weight_ref[...], preferred_element_type=jnp.float32
    )
    product_ref[...] = product.astype(jnp.bfloat16).reshape(product_ref.shape)


IN_SMEM = pl.BlockSpec(memory_space=pltpu.SMEM)
IN_VMEM = pl.BlockSpec(memory_space=pltpu.VMEM)
ANYWHERE = pl.BlockSpec(memory_space=pl.ANY)


def after(value, *others):
    return lax.optimization_barrier((value,) + others)[0]


def parts_to_patch_owners(block):
    frames_each, patches_here, width = block.shape[1:]
    owners = lax.axis_size("tm")
    part = jax.ShapeDtypeStruct((patches_here // owners, frames_each, width), block.dtype)
    parts = pl.pallas_call(
        split_kernel,
        in_specs=[IN_SMEM, IN_VMEM],
        out_specs=[IN_VMEM] * owners,
        out_shape=[part] * owners,
        compiler_params=pltpu.CompilerParams(vmem_limit_bytes=VMEM_BYTES),
        cost_estimate=pl.CostEstimate(flops=2 * 64 * block.size, bytes_accessed=4 * block.size, transcendentals=0),
    )(lax.axis_index("tm").reshape(1), block.reshape(frames_each, owners, patches_here // owners, width))
    steps = far_first(owners)
    return [parts[0]] + [shift_over(parts[step], "tm", step) for step in steps], (0, *steps)


def join_and_normalize(parts, steps):
    owners = len(parts)
    whole = jax.ShapeDtypeStruct((owners,) + parts[0].shape, jnp.bfloat16)
    return pl.pallas_call(
        functools.partial(join_kernel, steps),
        in_specs=[IN_SMEM] + [ANYWHERE] * owners,
        out_specs=[IN_VMEM, IN_VMEM],
        out_shape=[whole, whole],
        scratch_shapes=[pltpu.SemaphoreType.DMA((owners,))],
        compiler_params=pltpu.CompilerParams(vmem_limit_bytes=VMEM_BYTES),
        cost_estimate=pl.CostEstimate(flops=8 * whole.size, bytes_accessed=6 * whole.size, transcendentals=512),
    )(lax.axis_index("tm").reshape(1), *parts)


def project(parts, steps, gathered, first, columns):
    owners = len(parts)
    patches_each, frames_each, width = parts[0].shape
    token_shape = (owners, patches_each, frames_each)
    block = 768
    return pl.pallas_call(
        functools.partial(project_kernel, steps),
        grid=(columns // block,),
        in_specs=[IN_SMEM]
        + [ANYWHERE] * owners
        + [pl.BlockSpec((width, block), lambda j: (0, j + first // block))],
        out_specs=[
            pl.BlockSpec(token_shape + (width,), lambda j: (0, 0, 0, 0)),
            pl.BlockSpec(token_shape + (block,), lambda j: (0, 0, 0, j)),
        ],
        out_shape=[
            jax.ShapeDtypeStruct(token_shape + (width,), jnp.bfloat16),
            jax.ShapeDtypeStruct(token_shape + (columns,), jnp.bfloat16),
        ],
        scratch_shapes=[pltpu.SemaphoreType.DMA((owners,))],
        compiler_params=pltpu.CompilerParams(vmem_limit_bytes=VMEM_BYTES),
        cost_estimate=pl.CostEstimate(
            flops=2 * 512 * width * columns, bytes_accessed=2 * width * columns, transcendentals=0
        ),
    )(lax.axis_index("tm").reshape(1), *parts, gathered)


def in_frames(back):
    owners, patches_each, frames_each, width = back.shape
    return back.transpose(2, 0, 1, 3).reshape(1, frames_each, owners * patches_each, width)


def attention_mask(frame_time, senders, frames_each):
    rows = np.arange(senders * 2 * frames_each)
    patch = (rows // frames_each) % 2
    frame = (rows // (2 * frames_each)) * frames_each + rows % frames_each
    times = frame_time[0][frame]
    allowed = (times[None, :] <= times[:, None]) & (patch[None, :] == patch[:, None])
    allowed = allowed.astype(jnp.float32)
    return jnp.concatenate([allowed, allowed], axis=0)


def rounded_sum(*values):
    total = values[0].astype(jnp.float32)
    for value in values[1:]:
        total = total + value.astype(jnp.float32)
    return total.astype(jnp.bfloat16)


def pick(value, index, axis):
    return lax.dynamic_index_in_dim(value, index, axis, keepdims=False)


def core_swap(term):
    y_count, x_count, cores = (lax.axis_size(axis) for axis in FSDP)
    core = lax.axis_index("core")
    rows = term.shape[0] // (y_count * x_count * cores)
    split = term.reshape(y_count, x_count, cores, rows, term.shape[1])
    return pick(split, core, 2), shift_over(pick(split, 1 - core, 2), "core", 1)


def x_first_step(both):
    opposite = pick(both, (lax.axis_index("x") + 2) % 4, 1)
    half = opposite.shape[1] // 2
    return shift_over(opposite[:, :half], "x", 1), shift_over(opposite[:, half:], "x", -1)


def x_second_parts(both, from_left, from_right):
    x = lax.axis_index("x")
    half = both.shape[2] // 2
    up, down = pick(both, (x + 1) % 4, 1), pick(both, (x + 3) % 4, 1)
    up = jnp.concatenate([rounded_sum(up[:, :half], from_left), up[:, half:]], axis=1)
    down = jnp.concatenate([down[:, :half], rounded_sum(down[:, half:], from_right)], axis=1)
    return up, down


def x_second_step(up, down):
    return shift_over(up, "x", 1), shift_over(down, "x", -1)


def x_own(both):
    return pick(both, lax.axis_index("x"), 1)


def y_swap(column):
    y = lax.axis_index("yl")
    return pick(column, y, 0), shift_over(pick(column, 1 - y, 0), "yl", 1)


def sum_part_over_group(shard):
    count = lax.axis_size("pair") * lax.axis_size("tm")
    parts = shard.reshape(count, -1, 128)
    received = lax.all_to_all(parts, GROUP, split_axis=0, concat_axis=0, tiled=True)
    return jnp.sum(received.astype(jnp.float32), axis=0).astype(jnp.bfloat16)


def spread_over_group(part):
    count = lax.axis_size("pair") * lax.axis_size("tm")
    spread = jnp.broadcast_to(part[None], (count,) + part.shape)
    return lax.all_to_all(spread, GROUP, split_axis=0, concat_axis=0, tiled=True)


def on_device(frames, frame_time, w_qkv, w_out, grad_out):
    inner = w_out.shape[0]
    width = frames.shape[-1]
    gathered = lax.all_gather(
        jnp.concatenate([w_qkv, w_out.T], axis=1), FSDP, axis=0, tiled=True
    )
    full_qkv = gathered[:, : 3 * inner]
    token_parts, steps = parts_to_patch_owners(frames)
    grad_parts, steps = parts_to_patch_owners(grad_out)
    tokens, normed = join_and_normalize(token_parts, steps)
    token_shape = tokens.shape
    senders, patches_each, frames_each = token_shape[:3]
    mask = attention_mask(frame_time, senders, frames_each)

    float_rows = tokens.reshape(-1, width).astype(jnp.float32)
    inv_rms = lax.rsqrt(jnp.mean(float_rows * float_rows, axis=-1, keepdims=True) + 1e-06)
    normed = normed.reshape(-1, width)
    normed = after(normed, inv_rms)
    qkv = jnp.dot(normed, full_qkv, preferred_element_type=jnp.float32).astype(jnp.bfloat16)
    qkv = qkv.reshape(token_shape[:3] + (3 * inner,))
    mixed, weights = attention_forward(qkv, mask, inner)

    grad_tokens, d_mixed = project(grad_parts, steps, gathered, 3 * inner, inner)
    grad_rows = grad_tokens.reshape(-1, width)
    d_qkv = attention_backward(qkv, d_mixed, weights)
    d_rows = d_qkv.reshape(-1, 3 * inner)

    cut = 3 * inner // 2
    first_term = contract(normed, d_rows[:, :cut], 0, 0).astype(jnp.bfloat16)
    first_keep, first_swapped = core_swap(first_term)
    second_term = contract(normed, after(d_rows, first_term)[:, cut:], 0, 0).astype(jnp.bfloat16)
    second_keep, second_swapped = core_swap(second_term)
    both_first = rounded_sum(first_keep, after(first_swapped, second_term))
    first_left, first_right = x_first_step(both_first)
    both_second = rounded_sum(second_keep, after(second_swapped, both_first))
    second_own, second_moved = y_swap(both_second)
    mixed_rows = after(mixed.reshape(-1, inner), both_second)
    term_out = contract(grad_rows, mixed_rows, 0, 0).astype(jnp.bfloat16)
    out_keep, out_swapped = core_swap(term_out)

    d_rows, grad_rows = lax.optimization_barrier((d_rows, grad_rows, term_out))[:2]
    d_normed = contract(d_rows, full_qkv, 1, 1)
    scaled = float_rows * inv_rms
    inner_term = jnp.mean(d_normed * scaled, axis=-1, keepdims=True)
    grad_local = grad_rows.astype(jnp.float32) + inv_rms * (d_normed - scaled * inner_term)
    grad_local = grad_local.astype(jnp.bfloat16).reshape(token_shape)
    grad_back = lax.all_to_all(grad_local, "tm", split_axis=0, concat_axis=0, tiled=True)

    first_left, first_right, out_swapped = lax.optimization_barrier(
        (first_left, first_right, out_swapped, grad_local)
    )[:3]
    up, down = x_second_parts(both_first, first_left, first_right)
    first_moved = x_second_step(up, down)
    out_swapped, second_moved = lax.optimization_barrier((out_swapped, second_moved, up, down))[:2]
    both_out = rounded_sum(out_keep, out_swapped)
    out_parts = x_second_parts(both_out, *x_first_step(both_out))
    shard_out = rounded_sum(*y_swap(rounded_sum(x_own(both_out), *x_second_step(*out_parts))))

    column = rounded_sum(second_own, second_moved)[None]
    column_moved = x_second_step(*x_second_parts(column, *x_first_step(column)))
    shard_first = rounded_sum(*y_swap(rounded_sum(x_own(both_first), *first_moved)))
    shard_second = rounded_sum(x_own(column), *column_moved)[0]
    shards = jnp.concatenate([shard_first, shard_second, shard_out], axis=1)
    part = sum_part_over_group(after(shards, grad_back))
    grad_frames = in_frames(after(grad_back, part))
    summed = spread_over_group(part).reshape(shards.shape).astype(jnp.float32)
    summed_qkv, summed_out = summed[:, : 3 * inner], summed[:, 3 * inner :]
    tokens_all = frames.shape[0] * frames.shape[1] * frames.shape[2]
    for axis in GROUP + FSDP:
        tokens_all *= lax.axis_size(axis)
    grad_scale = 1.0 / math.sqrt(tokens_all)
    return (grad_frames, summed_qkv * grad_scale, summed_out.T * grad_scale)


def solution(mesh):
    pairs, times, shards = (mesh.shape[name] for name in ("pair", "tm", "fsdp"))
    cut = Mesh(
        mesh.devices.reshape(pairs, times, 2, shards // 4, 2), ("pair", "tm") + FSDP
    )
    tokens_spec = P("pair", "tm", FSDP, None)
    return jax.shard_map(
        on_device,
        mesh=cut,
        in_specs=(tokens_spec, P("pair", None), P(FSDP, None), P(None, FSDP), tokens_spec),
        out_specs=(tokens_spec, P(FSDP, None), P(None, FSDP)),
        check_vma=False,
    )
```
